256 devices in a mesh: leaf: 64 (over z, x, core), sub: 4 (over y).
Axes of the slice: x: 4, y: 4, z: 8, core: 2. Of those that a mesh axis runs over, the one named last changes fastest.
Arguments:
- vectors: bfloat16 [32, 262144], P(None, ('leaf', 'sub')), may hold values from -6 to 6
- right_side: bfloat16 [32, 262144], P(None, ('leaf', 'sub')), may hold values from -6 to 6
- tree_order: int32 [256, 1024], P(('leaf', 'sub')), may hold values from 0 to 1023, each once within a row
- live_counts: int32 [256], P(('leaf', 'sub')), may hold values from 1 to 1024, 196608 in all
- leaf_block: bfloat16 [262144, 1024], P(('leaf', 'sub')), may hold values from -0.1875 to 0.1875
- left_basis: bfloat16 [8, 262144, 128], P(None, ('leaf', 'sub')), may hold values from -0.5 to 0.5
- right_level_bases: bfloat16 [8, 262144, 128], P(None, ('leaf', 'sub')), may hold values from -0.1875 to 0.1875
- coupling: bfloat16 [256, 8, 256, 128], P(('leaf', 'sub')), may hold values from -0.375 to 0.375
Outputs:
- product: float32 [32, 262144], P(None, ('leaf', 'sub'))
- solution: float32 [32, 262144], P(None, ('leaf', 'sub'))
The draws below stay inside these ranges and needn't reach their ends.
Inputs may be any that keep to these rules, and one draw needn't show every extreme that they name: `tree_order`: each row is a permutation of 0 to 1023. `live_counts`: the counts sum to 196608, the largest is exactly 1024.
All inputs are finite; a program needn't handle non-finite values. No bound on the sum of `live_counts` on one device may be relied on, other than what follows from the above.
Results may differ from the reference program's by a relative error of at most 0.028.
Values may be sent and summed in bfloat16 or wider, within the bound.
No kernel may reach another device: no remote copies, remote signals or barrier semaphores. Data moves between devices by JAX's collectives and lax.ppermute only.
A program may use at most 64 MiB of HBM per device.

```python
import math
import jax
import jax.numpy as jnp
import numpy as np
from jax import lax

LEAF = 1024
RANK = 128
NVEC = 32
LEAVES = 256
POINTS = 262144
LEVELS = 8


def level_of(rng, extent, cuts, least, high):
    level, own = 1.0, jax.random.fold_in(rng, 6)
    for axis_at, shards_of in cuts:
        steps = jnp.exp(jax.random.uniform(jax.random.fold_in(own, axis_at), (shards_of,), jnp.float32, least / len(cuts), high / len(cuts)))
        level = level * jnp.repeat(steps, extent[axis_at] // shards_of).reshape([-1 if axis == axis_at else 1 for axis in range(len(extent))])
    return level


def profile(count, total, reach, slope):
    weights = [(1 << 20) // math.isqrt(rank ** slope) + 1 for rank in range(2, count + 1)]
    rest, holding = total - reach - (count - 1), [1] * (count - 1)
    while rest > 0:
        free = [i for i in range(count - 1) if holding[i] < reach]
        mass, remaining = sum([weights[i] for i in free]), rest
        for i in free:
            extra = min(reach - holding[i], max(1, remaining * weights[i] // mass), rest)
            holding[i] = holding[i] + extra
            rest = rest - extra
    return np.array([reach] + holding)


def ragged(stream_key, number_of, total, most, slope):
    if number_of == 2:
        one = jax.random.randint(stream_key, (), max(1, total - most), min(most, total - 1) + 1)
        return jnp.stack([one, total - one])
    sizes = jnp.asarray(profile(number_of, total, most, slope), jnp.int32)
    pairs = (number_of - 1) // 2
    source_of, sink = sizes[1:1 + 2 * pairs:2], sizes[2:2 + 2 * pairs:2]
    slack = jnp.minimum(source_of - 1, most - sink)
    passed = jax.random.randint(jax.random.fold_in(stream_key, 1), (pairs,), 0, 1 << 20) % (slack + 1)
    sizes = sizes.at[1:1 + 2 * pairs:2].set(source_of - passed).at[2:2 + 2 * pairs:2].set(sink + passed)
    return sizes[jax.random.permutation(jax.random.fold_in(stream_key, 2), number_of)]


def gaussian(rng, extent, deviation, reach, cuts=(), held_as=jnp.bfloat16):
    drawn = deviation * jax.random.normal(rng, extent, jnp.float32)
    if cuts:
        drawn = drawn * level_of(rng, extent, cuts, -0.22, 0.18)
    return jnp.clip(drawn, -reach, reach).astype(held_as)


def setup_inputs(seed: int = 0) -> dict:
    key_list = jax.random.split(jax.random.key(seed), 9)
    vectors = gaussian(key_list[0], (NVEC, POINTS), 1.0, 6.0, ((1, 256),))
    right_side = gaussian(key_list[1], (NVEC, POINTS), 1.0, 6.0, ((1, 256),))
    tree_order = jax.vmap(lambda own: jax.random.permutation(own, LEAF))(jax.random.split(key_list[2], LEAVES)).reshape((LEAVES, LEAF)).astype(jnp.int32)
    live_counts = ragged(key_list[3], LEAVES, LEAVES * LEAF * 3 // 4, LEAF, 0).astype(jnp.int32)
    leaf_block = gaussian(key_list[4], (POINTS, LEAF), LEAF ** -0.5, 0.1875, ((0, 256),))
    left_basis = gaussian(key_list[5], (LEVELS, POINTS, RANK), RANK ** -0.5, 0.5, ((1, 256),))
    right_level_bases = gaussian(key_list[6], (LEVELS, POINTS, RANK), LEAF ** -0.5, 0.1875, ((1, 256),))
    coupling = gaussian(key_list[7], (LEAVES, LEVELS, 2 * RANK, RANK), (2 * RANK) ** -0.5, 0.375, ((0, 256),))
    return dict(vectors=vectors, right_side=right_side, tree_order=tree_order, live_counts=live_counts, leaf_block=leaf_block, left_basis=left_basis, right_level_bases=right_level_bases, coupling=coupling)


def to_tree(values_in, tree_order, live_counts):
    leaves = values_in.reshape(NVEC, LEAVES, LEAF).transpose(1, 0, 2)
    indices = jnp.broadcast_to(tree_order[:, None, :], leaves.shape)
    moved = jnp.take_along_axis(leaves, indices, axis=2)
    live_mask = lax.broadcasted_iota(jnp.int32, (LEAVES, 1, LEAF), 2) < live_counts[:, None, None]
    return jnp.where(live_mask, moved, jnp.zeros((), moved.dtype)), live_mask


def from_tree(values_in, tree_order):
    inverse = jnp.argsort(tree_order, axis=1).astype(jnp.int32)
    indices = jnp.broadcast_to(inverse[:, None, :], values_in.shape)
    back = jnp.take_along_axis(values_in, indices, axis=2)
    return back.transpose(1, 0, 2).reshape(NVEC, LEAVES * LEAF)


def leaf_coefficients(tree_field, basis):
    blocks = basis.reshape(LEAVES, LEAF, RANK).astype(jnp.float32)
    return jnp.einsum('lvp,lpr->lvr', tree_field.astype(jnp.float32), blocks)


def pair_sums(expansion_weights, tree_height):
    group_extent = 2 ** tree_height
    nodes = LEAVES // (2 * group_extent)
    sums = expansion_weights.reshape(nodes, 2, group_extent, NVEC, RANK).sum(axis=2) * (group_extent ** -0.5)
    shape_out = (nodes, 2, group_extent, NVEC, RANK)
    mine_sum = jnp.broadcast_to(sums[:, :, None], shape_out).reshape(LEAVES, NVEC, RANK)
    other_sum = jnp.broadcast_to(sums[:, ::-1, None], shape_out).reshape(LEAVES, NVEC, RANK)
    return mine_sum, other_sum


def expand(expansion_weights, basis):
    blocks = basis.reshape(LEAVES, LEAF, RANK).astype(jnp.float32)
    return jnp.einsum('lvr,lpr->lvp', expansion_weights.astype(jnp.float32), blocks)


def reference(vectors, right_side, tree_order, live_counts, leaf_block, left_basis, right_level_bases, coupling):
    tree_x, live_mask = to_tree(vectors, tree_order, live_counts)
    blocks = leaf_block.reshape(LEAVES, LEAF, LEAF)

    def dense_leaf(pieces):
        return jnp.dot(pieces[0], pieces[1].T, preferred_element_type=jnp.float32)

    total = lax.map(dense_leaf, (tree_x, blocks))
    for tree_height in range(LEVELS):
        expansion_weights = leaf_coefficients(tree_x, right_level_bases[tree_height])
        mine_sum, other_sum = pair_sums(expansion_weights, tree_height)
        total = total + expand(other_sum.astype(jnp.bfloat16), left_basis[tree_height])
    total = jnp.where(live_mask, total, jnp.float32(0.0))
    product = from_tree(total, tree_order)

    state, live_mask = to_tree(right_side, tree_order, live_counts)
    state = state.astype(jnp.float32)
    link_every_level = coupling.astype(jnp.float32)
    for tree_height in range(LEVELS):
        expansion_weights = leaf_coefficients(state.astype(jnp.bfloat16), right_level_bases[tree_height])
        mine_sum, other_sum = pair_sums(expansion_weights, tree_height)
        merged_result = jnp.concatenate([mine_sum, other_sum], axis=2).astype(jnp.bfloat16)
        linked_result = jnp.einsum('igo,ioa->iga', merged_result.astype(jnp.float32), link_every_level[:, tree_height]).astype(jnp.bfloat16)
        state = jnp.where(live_mask, state - expand(linked_result, left_basis[tree_height]), jnp.float32(0.0))
    solution = from_tree(state, tree_order)
    return product, solution
```

```python
import functools

import jax
import jax.numpy as jnp
from jax import lax
from jax.experimental import pallas as pl
from jax.experimental.pallas import tpu as pltpu
from jax.sharding import PartitionSpec as P

BF = jnp.bfloat16
F32 = jnp.float32
LANE = 128
VMEM = pl.BlockSpec(memory_space=pltpu.VMEM)
SMEM = pl.BlockSpec(memory_space=pltpu.SMEM)
HBM = pl.BlockSpec(memory_space=pl.ANY)
NT = (((1,), (1,)), ((), ()))
LEVELS = 8
SUMMED = 3


def scale(level):
    return 2.0 ** (-0.5 * level)


def dot(a, b):
    return jnp.dot(a, b, preferred_element_type=F32)


def dot_t(a, b):
    return lax.dot_general(a, b, NT, preferred_element_type=F32)


def one_hot(order, low, width):
    rows = lax.broadcasted_iota(jnp.int32, (order.shape[1], width), 0)
    return jnp.where(rows == order[:, low : low + width], 1.0, 0.0).astype(BF)


def columns(ref, level):
    return ref.at[:, pl.ds(level * LANE, LANE)]


def coefficient_kernel(live, order, vec, rhs, right, first_out, solve_out, tree_out, right_cat, tree, sems):
    copies = [
        pltpu.make_async_copy(right.at[level], columns(right_cat, level), sems.at[level])
        for level in range(LEVELS)
    ]
    for copy in copies:
        copy.start()
    points = vec.shape[1]
    nvec = vec.shape[0]
    fields = jnp.concatenate([vec[...], rhs[...]], axis=0)
    chunk = 256
    for low in range(0, points, chunk):
        moved = dot(fields, one_hot(order[...], low, chunk))
        slot = lax.broadcasted_iota(jnp.int32, moved.shape, 1) + low
        tree[:, low : low + chunk] = jnp.where(slot < live[0], moved, 0.0).astype(BF)
    tree_out[...] = tree[:nvec, :]
    for copy in copies:
        copy.wait()
    for level in range(0, LEVELS, 2):
        pair = dot(tree[...], right_cat[:, level * LANE : (level + 2) * LANE])
        for now in (level, level + 1):
            part = pair[:, (now - level) * LANE : (now - level + 1) * LANE] * scale(now)
            first_out[:, (now + 1) * LANE : (now + 2) * LANE] = part[:nvec].astype(BF)
            if now == 0:
                first_out[:, :LANE] = part[nvec:].astype(BF)
            else:
                solve_out[:, (now - 1) * LANE : now * LANE] = part[nvec:]


def update_kernel(live, index, coupling, left, right, *rest):
    outs, (right_cat, left_cat, sems) = rest[:-3], rest[-3:]
    rights = [
        pltpu.make_async_copy(right.at[level], columns(right_cat, level - 1), sems.at[0, level])
        for level in range(1, LEVELS)
    ]
    lefts = [
        pltpu.make_async_copy(left.at[level], columns(left_cat, level), sems.at[1, level])
        for level in range(LEVELS - 1)
    ]
    for copy in rights + lefts:
        copy.start()
    for copy in rights:
        copy.wait()
    at = 0
    for level in range(LEVELS - 1):
        lefts[level].wait()
        block = left_cat[:, level * LANE : (level + 1) * LANE]
        rows = lax.broadcasted_iota(jnp.int32, block.shape, 0)
        block = jnp.where(rows < live[0], block.astype(F32), 0.0)
        turned = block.T.astype(BF)
        gram = dot(turned, right_cat[:, level * LANE :])
        gram = jnp.concatenate(
            [
                (gram[:, (now - level - 1) * LANE : (now - level) * LANE] * scale(now)).astype(BF)
                for now in range(level + 1, LEVELS)
            ],
            axis=1,
        )
        update = dot(canonical(coupling, index, level), gram).astype(BF)
        if level < SUMMED:
            outs[level][...] = update
        else:
            width = update.shape[1]
            outs[SUMMED][:, at : at + width] = update
            at += width


def canonical(coupling, index, level):
    held = coupling[level]
    swapped = jnp.concatenate([held[LANE:], held[:LANE]], axis=0)
    second = (lax.shift_right_logical(index[0], level) & 1) == 1
    return jnp.where(second, swapped, held)


def local_kernel(live, order, tree_x, rhs, block, left, prod_out, sol_out, moved_out, block_in, left_cat, hot, sems):
    copies = [
        pltpu.make_async_copy(left.at[level], columns(left_cat, level), sems.at[level])
        for level in range(LEVELS)
    ]
    block_copy = pltpu.make_async_copy(block, block_in, sems.at[LEVELS])
    block_copy.start()
    for copy in copies:
        copy.start()
    points = order.shape[1]
    chunk = 256
    for low in range(0, points, chunk):
        hot[:, low : low + chunk] = one_hot(order[...], low, chunk)
    slot = lax.broadcasted_iota(jnp.int32, (8, points), 1)
    alive = jnp.where(slot < live[0], 1.0, 0.0).astype(BF)
    kept = dot_t(alive, hot[...])
    sol_out[...] = rhs[...].astype(F32) * kept[:1]
    block_copy.wait()
    direct = dot_t(tree_x[...], block_in[...])
    slot = lax.broadcasted_iota(jnp.int32, direct.shape, 1)
    direct = jnp.where(slot < live[0], direct, 0.0)
    high = direct.astype(BF)
    low_part = (direct - high.astype(F32)).astype(BF)
    prod_out[...] = dot_t(high, hot[...]) + dot_t(low_part, hot[...])
    for copy in copies:
        copy.wait()
    for low in range(0, LEVELS * LANE, chunk):
        part = left_cat[:, low : low + chunk]
        rows = lax.broadcasted_iota(jnp.int32, part.shape, 0)
        part = jnp.where(rows < live[0], part.astype(F32), 0.0).astype(BF)
        moved_out[:, low : low + chunk] = dot(hot[...], part).astype(BF)


def partial_kernel(index, coupling, moved, prod, sol, siblings, joined, prod_out, sol_out):
    count = LEVELS - 1
    moved_now = moved[:, : count * LANE]
    prod_out[...] = prod[...] + dot_t(siblings[...], moved_now)
    coupled = [
        dot(joined[:, 2 * level * LANE : 2 * (level + 1) * LANE], canonical(coupling, index, level)).astype(BF)
        for level in range(count)
    ]
    sol_out[...] = sol[...] - dot_t(jnp.concatenate(coupled, axis=1), moved_now)


def last_kernel(index, coupling, moved, prod, sol, sibling, joined, prod_out, sol_out):
    prod_out[...] = prod[...] + dot_t(sibling[...], moved[...])
    held = coupling[...]
    swapped = jnp.concatenate([held[LANE:], held[:LANE]], axis=0)
    second = (lax.shift_right_logical(index[0], LEVELS - 1) & 1) == 1
    coupled = dot(joined[...], jnp.where(second, swapped, held)).astype(BF)
    sol_out[...] = sol[...] - dot_t(coupled, moved[...])


def params(mib):
    return pltpu.CompilerParams(vmem_limit_bytes=mib << 20)


def shape(rows, lanes, dtype=BF):
    return jax.ShapeDtypeStruct((rows, lanes), dtype)


def swap(block, mask):
    count = lax.axis_size("leaf") * lax.axis_size("sub")
    return lax.ppermute(block, ("leaf", "sub"), [(i, i ^ mask) for i in range(count)])


def cols(block, low, high=None):
    return block[:, low * LANE : None if high is None else high * LANE]


def cat(*blocks):
    return jnp.concatenate([block.astype(BF) for block in blocks], axis=1)


def per_device(vectors, right_side, tree_order, live_counts, leaf_block, left_basis, right_bases, coupling):
    nvec, points = vectors.shape
    index = lax.axis_index("leaf") * lax.axis_size("sub") + lax.axis_index("sub")
    index_1 = index.astype(jnp.int32).reshape(1)
    sub, core = index & 3, (index >> 2) & 1
    coupling = coupling[0]

    def join(mine, other, level):
        second = ((index >> level) & 1) == 1
        return cat(jnp.where(second, other, mine), jnp.where(second, mine, other))

    first, coef, tree_x = pl.pallas_call(
        coefficient_kernel,
        out_shape=(shape(nvec, 9 * LANE), shape(nvec, 7 * LANE, F32), shape(nvec, points)),
        in_specs=[SMEM, VMEM, VMEM, VMEM, HBM],
        out_specs=(VMEM, VMEM, VMEM),
        scratch_shapes=[
            pltpu.VMEM((points, LEVELS * LANE), BF),
            pltpu.VMEM((2 * nvec, points), BF),
            pltpu.SemaphoreType.DMA((LEVELS,)),
        ],
        compiler_params=params(24),
        cost_estimate=pl.CostEstimate(flops=300_000_000, bytes_accessed=2_500_000, transcendentals=0),
        name="coefficients",
    )(live_counts, tree_order, vectors, right_side, right_bases)

    widths = [LEVELS - 1 - level for level in range(SUMMED)]
    summed = sum(LEVELS - 1 - level for level in range(SUMMED, LEVELS - 1))
    update_0, update_1, update_2, update_up = pl.pallas_call(
        update_kernel,
        out_shape=tuple(shape(2 * LANE, width * LANE) for width in widths + [summed]),
        in_specs=[SMEM, SMEM, VMEM, HBM, HBM],
        out_specs=(VMEM,) * 4,
        scratch_shapes=[
            pltpu.VMEM((points, 7 * LANE), BF),
            pltpu.VMEM((points, 7 * LANE), BF),
            pltpu.SemaphoreType.DMA((2, LEVELS)),
        ],
        compiler_params=params(24),
        cost_estimate=pl.CostEstimate(flops=1_300_000_000, bytes_accessed=5_000_000, transcendentals=0),
        name="updates",
    )(live_counts, index_1, coupling, left_basis, right_bases)

    base_prod, base_sol, moved = pl.pallas_call(
        local_kernel,
        out_shape=(shape(nvec, points, F32), shape(nvec, points, F32), shape(points, LEVELS * LANE)),
        in_specs=[SMEM, VMEM, VMEM, VMEM, HBM, HBM],
        out_specs=(VMEM, VMEM, VMEM),
        scratch_shapes=[
            pltpu.VMEM((points, points), BF),
            pltpu.VMEM((points, LEVELS * LANE), BF),
            pltpu.VMEM((points, points), BF),
            pltpu.SemaphoreType.DMA((LEVELS + 1,)),
        ],
        compiler_params=params(32),
        cost_estimate=pl.CostEstimate(flops=2_500_000_000, bytes_accessed=7_000_000, transcendentals=0),
        name="local",
    )(live_counts, tree_order, tree_x, right_side, leaf_block, left_basis)

    siblings, joined = [], []

    got = swap(first, 1)
    joined.append(join(cols(first, 0, 1), cols(got, 0, 1), 0))
    siblings.append(cols(got, 1, 2))
    prod = cols(first, 2).astype(F32) + cols(got, 2).astype(F32)
    coef = coef - dot(joined[0], update_0)

    half = update_up.shape[0] // 2
    away = lax.dynamic_slice_in_dim(update_up, (1 - core) * half, half, 0)
    home = lax.dynamic_slice_in_dim(update_up, core * half, half, 0)
    halves = (home.astype(F32) + swap(away, 4).astype(F32)).astype(BF)
    piece = half // 4

    def rows_of(mask):
        return lax.dynamic_slice_in_dim(halves, (sub ^ mask) * piece, piece, 0)

    mine = cols(coef, 0, 1)
    got = {
        1: swap(cat(mine, rows_of(1)), 1),
        2: swap(cat(mine, rows_of(2)), 2),
        3: swap(cat(mine, rows_of(3), prod), 3),
    }
    parts = {mask: cols(block, 0, 1).astype(F32) for mask, block in got.items()}
    joined.append(join((mine + parts[1]).astype(BF), (parts[2] + parts[3]).astype(BF), 1))
    pieces = rows_of(0).astype(F32)
    for mask in (1, 2, 3):
        pieces = pieces + cols(got[mask], 1, 1 + summed).astype(F32)
    got_prod = cols(got[3], 1 + summed)
    siblings.append(cols(got_prod, 0, 1))
    prod = cols(prod, 1) + cols(got_prod, 1).astype(F32)
    coef = cols(coef, 1) - dot(joined[1], update_1)

    sent = coef.astype(BF)
    pieces_3 = pieces + swap(pieces.astype(BF), 8).astype(F32)
    total = coef
    for mask in (1, 2, 3):
        total = total + swap(sent, mask).astype(F32)
    pieces_4 = cols(pieces_3, 4) + swap(cols(pieces_3, 4).astype(BF), 24).astype(F32)
    got = swap(cat(total, prod), 4)
    got_total, got_prod = cols(got, 0, 6), cols(got, 6)
    joined.append(join(cols(total, 0, 1).astype(BF), cols(got_total, 0, 1), 2))
    siblings.append(cols(got_prod, 0, 1))
    total = cols(total, 1) + cols(got_total, 1).astype(F32)
    prod = cols(prod, 1) + cols(got_prod, 1).astype(F32)
    change = dot(joined[2], update_2)

    def gather_rows(block, extra):
        sent = cat(extra, block) if extra is not None else block.astype(BF)
        lead = extra.shape[1] if extra is not None else 0
        got = {mask: swap(sent, mask) for mask in (1, 2, 3)}
        blocks = {0: block.astype(BF)}
        for mask in (1, 2, 3):
            blocks[mask] = got[mask][:, lead:]
            if extra is not None:
                extra = extra + got[mask][:, :lead].astype(F32)
        odd, high = (sub & 1) == 1, (sub >> 1) == 1
        low_pair = [jnp.where(odd, blocks[1], blocks[0]), jnp.where(odd, blocks[0], blocks[1])]
        high_pair = [jnp.where(odd, blocks[3], blocks[2]), jnp.where(odd, blocks[2], blocks[3])]
        ordered = [jnp.where(high, b, a) for a, b in zip(low_pair, high_pair)]
        ordered += [jnp.where(high, a, b) for a, b in zip(low_pair, high_pair)]
        return ordered, extra

    def gather_cores(ordered, extra):
        width = ordered[0].shape[1]
        lead = extra.shape[1] if extra is not None else 0
        got = swap(cat(*([extra] if extra is not None else []), *ordered), 4)
        theirs = [got[:, lead + i * width : lead + (i + 1) * width] for i in range(4)]
        mine, theirs = jnp.concatenate(ordered, axis=0), jnp.concatenate(theirs, axis=0)
        second = core == 1
        whole = jnp.concatenate([jnp.where(second, theirs, mine), jnp.where(second, mine, theirs)], axis=0)
        if extra is not None:
            extra = extra + got[:, :lead].astype(F32)
        return whole, extra

    ordered, change = gather_rows(cat(cols(pieces_3, 0, 4), cols(pieces_4, 0, 3)), change)
    whole, change = gather_cores(ordered, change)
    total = total - change
    summed_updates = {3: cols(whole, 0, 4), 4: cols(whole, 4)}
    pieces_5 = cols(pieces_4, 3) + swap(cols(pieces_4, 3).astype(BF), 32).astype(F32)
    pieces_6 = cols(pieces_5, 2) + swap(cols(pieces_5, 2).astype(BF), 64).astype(F32)
    ordered, _ = gather_rows(cat(cols(pieces_5, 0, 2), pieces_6), None)
    whole, _ = gather_cores(ordered, None)
    summed_updates[5], summed_updates[6] = cols(whole, 0, 2), cols(whole, 2)

    for level, mask in ((3, 8), (4, 24), (5, 32), (6, 64)):
        left_over = LEVELS - level
        got = swap(cat(total, prod), mask)
        got_total, got_prod = cols(got, 0, left_over), cols(got, left_over)
        joined.append(join(cols(total, 0, 1).astype(BF), cols(got_total, 0, 1), level))
        siblings.append(cols(got_prod, 0, 1))
        total = cols(total, 1) + cols(got_total, 1).astype(F32) - dot(joined[level], summed_updates[level])
        prod = cols(prod, 1) + cols(got_prod, 1).astype(F32)
    sent = cat(total, prod)
    got = swap(sent, 224)
    part_prod, part_sol = pl.pallas_call(
        partial_kernel,
        out_shape=(shape(nvec, points, F32),) * 2,
        in_specs=[SMEM] + [VMEM] * 6,
        out_specs=(VMEM, VMEM),
        compiler_params=params(16),
        cost_estimate=pl.CostEstimate(flops=150_000_000, bytes_accessed=3_000_000, transcendentals=0),
        name="partial",
    )(index_1, coupling, moved, base_prod, base_sol, cat(*siblings), cat(*joined))
    last_joined = join(cols(sent, 0, 1), cols(got, 0, 1), LEVELS - 1)
    return pl.pallas_call(
        last_kernel,
        out_shape=(shape(nvec, points, F32),) * 2,
        in_specs=[SMEM] + [VMEM] * 6,
        out_specs=(VMEM, VMEM),
        compiler_params=params(8),
        cost_estimate=pl.CostEstimate(flops=30_000_000, bytes_accessed=1_000_000, transcendentals=0),
        name="last",
    )(
        index_1,
        coupling[LEVELS - 1],
        cols(moved, LEVELS - 1),
        part_prod,
        part_sol,
        cols(got, 1),
        last_joined,
    )


def solution(mesh):
    placed = (
        P(None, ("leaf", "sub")),
        P(None, ("leaf", "sub")),
        P(("leaf", "sub"), None),
        P(("leaf", "sub")),
        P(("leaf", "sub"), None),
        P(None, ("leaf", "sub"), None),
        P(None, ("leaf", "sub"), None),
        P(("leaf", "sub"), None, None, None),
    )
    return jax.shard_map(
        per_device,
        mesh=mesh,
        in_specs=placed,
        out_specs=(P(None, ("leaf", "sub")), P(None, ("leaf", "sub"))),
        check_vma=False,
    )
```

```python
import functools

import jax
import jax.numpy as jnp
from jax import lax
from jax.experimental import pallas as pl
from jax.experimental.pallas import tpu as pltpu
from jax.sharding import PartitionSpec as P

BF = jnp.bfloat16
F32 = jnp.float32
LANE = 128
VMEM = pl.BlockSpec(memory_space=pltpu.VMEM)
SMEM = pl.BlockSpec(memory_space=pltpu.SMEM)
HBM = pl.BlockSpec(memory_space=pltpu.HBM)
NT = (((1,), (1,)), ((), ()))
LEVELS = 8
SUMMED = 3
BEFORE = 6


def scale(level):
    return 2.0 ** (-0.5 * level)


def dot(a, b):
    return jnp.dot(a, b, preferred_element_type=F32)


def dot_t(a, b):
    return lax.dot_general(a, b, NT, preferred_element_type=F32)


def one_hot(order, low, width):
    rows = lax.broadcasted_iota(jnp.int32, (order.shape[1], width), 0)
    return jnp.where(rows == order[:, low : low + width], 1.0, 0.0).astype(BF)


def columns(ref, level):
    return ref.at[:, pl.ds(level * LANE, LANE)]


def coefficient_kernel(
    live, order, vec, rhs, right, first_out, solve_out, tree_out, right_cat, fields, order_in, sems
):
    nvec = vec.shape[0]
    points = vec.shape[1]
    small = [
        pltpu.make_async_copy(order, order_in, sems.at[LEVELS]),
        pltpu.make_async_copy(vec, fields.at[pl.ds(0, nvec)], sems.at[LEVELS + 1]),
        pltpu.make_async_copy(rhs, fields.at[pl.ds(nvec, nvec)], sems.at[LEVELS + 2]),
    ]
    copies = [
        pltpu.make_async_copy(right.at[level], columns(right_cat, level), sems.at[level])
        for level in range(LEVELS)
    ]
    for copy in small + copies:
        copy.start()
    for copy in small:
        copy.wait()
    chunk = 256
    for low in range(0, points, chunk):
        moved = dot(fields[...], one_hot(order_in[...], low, chunk))
        slot = lax.broadcasted_iota(jnp.int32, moved.shape, 1) + low
        tree_out[:, low : low + chunk] = jnp.where(slot < live[0], moved, 0.0).astype(BF)
    for level in range(0, LEVELS, 2):
        copies[level].wait()
        copies[level + 1].wait()
        pair = dot(tree_out[...], right_cat[:, level * LANE : (level + 2) * LANE])
        for now in (level, level + 1):
            part = pair[:, (now - level) * LANE : (now - level + 1) * LANE] * scale(now)
            first_out[:, (now + 1) * LANE : (now + 2) * LANE] = part[:nvec].astype(BF)
            if now == 0:
                first_out[:, :LANE] = part[nvec:].astype(BF)
            else:
                solve_out[:, (now - 1) * LANE : now * LANE] = part[nvec:]


def update_kernel(live, index, coupling, left, right, *rest):
    outs, (right_cat, turned, left_cat, held, sems) = rest[: SUMMED + 3], rest[SUMMED + 3 :]
    home, away, bits = outs[SUMMED:]
    rights = {
        level: pltpu.make_async_copy(right.at[level], columns(right_cat, level - 1), sems.at[0, level])
        for level in range(1, LEVELS)
    }
    lefts = [
        pltpu.make_async_copy(left.at[level], columns(left_cat, level), sems.at[1, level])
        for level in range(LEVELS - 1)
    ]
    coupling_copy = pltpu.make_async_copy(coupling, held, sems.at[0, 0])
    for level in range(LEVELS - 1, 0, -1):
        rights[level].start()
    for copy in lefts[::-1]:
        copy.start()
    coupling_copy.start()
    levels = lax.broadcasted_iota(jnp.int32, bits.shape, 0)
    bits[...] = (lax.shift_right_logical(jnp.full(bits.shape, index[0], jnp.int32), levels) & 1).astype(F32)
    for level in range(LEVELS - 1, 0, -1):
        rights[level].wait()
        turned[(level - 1) * LANE : level * LANE, :] = right_cat[:, (level - 1) * LANE : level * LANE].T
    second_core = (lax.shift_right_logical(index[0], 2) & 1) == 1
    for low in range(LEVELS - 2, -1, -2):
        levels = [level for level in (low, low + 1) if level < LEVELS - 1]
        for level in levels[::-1]:
            lefts[level].wait()
        if low == LEVELS - 2:
            coupling_copy.wait()
        block = left_cat[:, low * LANE : (low + len(levels)) * LANE]
        rows = lax.broadcasted_iota(jnp.int32, block.shape, 0)
        block = jnp.where(rows < live[0], block.astype(F32), 0.0).astype(BF)
        gram = dot(turned[low * LANE :, :], block)
        for level in levels:
            side = slice((level - low) * LANE, (level - low + 1) * LANE)
            own = jnp.concatenate(
                [
                    (gram[(now - low - 1) * LANE : (now - low) * LANE, side] * scale(now)).astype(BF)
                    for now in range(level + 1, LEVELS)
                ],
                axis=0,
            )
            update = dot_t(canonical(held, index, level), own).astype(BF)
            if level < SUMMED:
                outs[level][...] = update
            else:
                at = sum(LEVELS - 1 - below for below in range(SUMMED, level)) * LANE
                to = slice(at, at + update.shape[1])
                first, second = update[:LANE], update[LANE:]
                home[:, to] = jnp.where(second_core, second, first)
                away[:, to] = jnp.where(second_core, first, second)


def canonical(coupling, index, level):
    held = coupling[level]
    swapped = jnp.concatenate([held[LANE:], held[:LANE]], axis=0)
    second = (lax.shift_right_logical(index[0], level) & 1) == 1
    return jnp.where(second, swapped, held)


def direct_kernel(live, order, tree, block, prod_out, hot_out):
    points = order.shape[1]
    nvec = prod_out.shape[0]
    chunk = 256
    for low in range(0, points, chunk):
        hot_out[:, low : low + chunk] = one_hot(order[...], low, chunk)
    prod_out[...] = dot_t(tree[:nvec, :], block[...])


def masked_rows(block, live):
    rows = lax.broadcasted_iota(jnp.int32, block.shape, 0)
    return jnp.where(rows < live[0], block.astype(F32), 0.0).astype(BF)


def moved_kernel(live, hot, left, moved_out, left_cat, sems):
    copies = [
        pltpu.make_async_copy(left.at[level], columns(left_cat, level - BEFORE), sems.at[level - BEFORE])
        for level in range(BEFORE, LEVELS)
    ]
    for copy in copies:
        copy.start()
    for copy in copies:
        copy.wait()
    moved_out[...] = dot(hot[...], masked_rows(left_cat[...], live)).astype(BF)


def partial_kernel(live, index, coupling, left, tree, direct, hot, *rest):
    siblings, joined = rest[:BEFORE], rest[BEFORE : 2 * BEFORE]
    prod_out, sol_out, coupling_out, left_cat, sems = rest[2 * BEFORE :]
    copies = [
        pltpu.make_async_copy(left.at[level], columns(left_cat, level), sems.at[level])
        for level in range(BEFORE)
    ]
    for copy in copies:
        copy.start()
    for level in range(BEFORE, LEVELS):
        at = (level - BEFORE) * 2 * LANE
        coupling_out[at : at + 2 * LANE, :] = canonical(coupling, index, level)
    coupled = [dot(joined[level][...], canonical(coupling, index, level)).astype(BF) for level in range(BEFORE)]
    siblings = [block[...] for block in siblings]
    terms = jnp.concatenate([jnp.concatenate(siblings, axis=1), jnp.concatenate(coupled, axis=1)], axis=0)
    for copy in copies:
        copy.wait()
    terms = dot_t(terms, left_cat[...])
    nvec = direct.shape[0]
    total = jnp.concatenate([direct[...] + terms[:nvec], tree[nvec:, :].astype(F32) - terms[nvec:]], axis=0)
    slot = lax.broadcasted_iota(jnp.int32, total.shape, 1)
    total = jnp.where(slot < live[0], total, 0.0)
    high = total.astype(BF)
    low = (total - high.astype(F32)).astype(BF)
    both = dot_t(jnp.concatenate([high, low], axis=0), hot[...])
    prod_out[...] = both[:nvec] + both[2 * nvec : 3 * nvec]
    sol_out[...] = both[nvec : 2 * nvec] + both[3 * nvec :]


def last_kernel(coupling, moved, prod, sol, *rest):
    count = LEVELS - BEFORE
    siblings, joined, (prod_out, sol_out) = rest[:count], rest[count : 2 * count], rest[2 * count :]
    coupled = [
        dot(joined[at][...], coupling[2 * at * LANE : 2 * (at + 1) * LANE, :]).astype(BF) for at in range(count)
    ]
    siblings = [block[...] for block in siblings]
    terms = jnp.concatenate([jnp.concatenate(siblings, axis=1), jnp.concatenate(coupled, axis=1)], axis=0)
    terms = dot_t(terms, moved[...])
    nvec = prod.shape[0]
    prod_out[...] = prod[...] + terms[:nvec]
    sol_out[...] = sol[...] - terms[nvec:]


def params(mib):
    return pltpu.CompilerParams(vmem_limit_bytes=mib << 20)


def shape(rows, lanes, dtype=BF):
    return jax.ShapeDtypeStruct((rows, lanes), dtype)


def swap(block, mask):
    count = lax.axis_size("leaf") * lax.axis_size("sub")
    return lax.ppermute(block, ("leaf", "sub"), [(i, i ^ mask) for i in range(count)])


def cols(block, low, high=None):
    return block[:, low * LANE : None if high is None else high * LANE]


def cat(*blocks):
    return jnp.concatenate([block.astype(BF) for block in blocks], axis=1)


def after(block, *others):
    return lax.optimization_barrier((block,) + others)[0]


def per_device(vectors, right_side, tree_order, live_counts, leaf_block, left_basis, right_bases, coupling):
    nvec, points = vectors.shape
    index = lax.axis_index("leaf") * lax.axis_size("sub") + lax.axis_index("sub")
    index_1 = index.astype(jnp.int32).reshape(1)
    coupling = coupling[0]

    def pick(level, if_set, if_clear):
        side = jnp.broadcast_to(bits[level : level + 1, : if_set.shape[1]], if_set.shape)
        return jnp.where(side > 0, if_set, if_clear)

    def join(mine, other, level):
        return cat(pick(level, other, mine), pick(level, mine, other))

    def whole_of(mine, theirs):
        width = mine.shape[1] // 4
        mine, theirs = (
            jnp.concatenate([half[:, at : at + width] for at in range(0, 4 * width, width)], axis=0)
            for half in (mine, theirs)
        )
        return jnp.concatenate([pick(2, theirs, mine), pick(2, mine, theirs)], axis=0)

    def by_sub(blocks):
        even = [pick(0, blocks[i ^ 1], blocks[i]) for i in range(4)]
        return [pick(1, even[i ^ 2], even[i]) for i in range(4)]

    first, coef, tree = pl.pallas_call(
        coefficient_kernel,
        out_shape=(
            shape(nvec, 9 * LANE),
            shape(nvec, 7 * LANE, F32),
            shape(2 * nvec, points),
        ),
        in_specs=[SMEM, HBM, HBM, HBM, HBM],
        out_specs=(VMEM,) * 3,
        scratch_shapes=[
            pltpu.VMEM((points, LEVELS * LANE), BF),
            pltpu.VMEM((2 * nvec, points), BF),
            pltpu.VMEM((1, points), jnp.int32),
            pltpu.SemaphoreType.DMA((LEVELS + 3,)),
        ],
        compiler_params=params(56),
        cost_estimate=pl.CostEstimate(flops=300_000_000, bytes_accessed=2_500_000, transcendentals=0),
        name="coefficients",
    )(after(live_counts, index_1), tree_order, vectors, right_side, right_bases)

    widths = [LEVELS - 1 - level for level in range(SUMMED)]
    summed = sum(LEVELS - 1 - level for level in range(SUMMED, LEVELS - 1))
    update_0, update_1, update_2, home, away, bits = pl.pallas_call(
        update_kernel,
        out_shape=tuple(shape(2 * LANE, width * LANE) for width in widths)
        + (shape(LANE, summed * LANE),) * 2
        + (shape(LEVELS, 2 * points, F32),),
        in_specs=[SMEM, SMEM, HBM, HBM, HBM],
        out_specs=(VMEM,) * 6,
        scratch_shapes=[
            pltpu.VMEM((points, 7 * LANE), BF),
            pltpu.VMEM((7 * LANE, points), BF),
            pltpu.VMEM((points, 7 * LANE), BF),
            pltpu.VMEM((LEVELS, 2 * LANE, LANE), BF),
            pltpu.SemaphoreType.DMA((2, LEVELS)),
        ],
        compiler_params=params(52),
        cost_estimate=pl.CostEstimate(flops=1_300_000_000, bytes_accessed=5_000_000, transcendentals=0),
        name="updates",
    )(live_counts, index_1, coupling, left_basis, right_bases)

    siblings, joined = [], []

    got = swap(first, 1)
    joined.append(join(cols(first, 0, 1), cols(got, 0, 1), 0))
    siblings.append(cols(got, 1, 2))
    prod = cols(first, 2).astype(F32) + cols(got, 2).astype(F32)
    coef = coef - dot(joined[0], update_0)

    halves = (home.astype(F32) + swap(away, 4).astype(F32)).astype(BF)
    piece = halves.shape[0] // 4
    rows_of = by_sub([halves[i * piece : (i + 1) * piece] for i in range(4)])

    mine = cols(coef, 0, 1).astype(BF)
    sent = {mask: cat(mine, rows_of[mask]) for mask in (1, 2, 3)}
    direct, hot = pl.pallas_call(
        direct_kernel,
        out_shape=(shape(nvec, points, F32), shape(points, points)),
        in_specs=[SMEM, VMEM, VMEM, VMEM],
        out_specs=(VMEM, VMEM),
        compiler_params=params(12),
        cost_estimate=pl.CostEstimate(flops=2_000_000_000, bytes_accessed=2_000_000, transcendentals=0),
        name="direct",
    )(after(live_counts, sent[3]), tree_order, tree, leaf_block)
    got = {mask: swap(sent[mask], mask) for mask in (1, 2, 3)}
    parts = {mask: cols(block, 0, 1).astype(F32) for mask, block in got.items()}
    pieces = rows_of[0].astype(F32)
    for mask in (1, 2, 3):
        pieces = pieces + cols(got[mask], 1).astype(F32)
    pieces = pieces.astype(BF)
    upper = cols(pieces, 4)
    near = swap(pieces, 8).astype(F32)
    upper = upper.astype(F32) + cols(near, 4) + swap(upper, 16).astype(F32) + swap(upper, 24).astype(F32)
    pieces = cat(cols(pieces, 0, 4).astype(F32) + cols(near, 0, 4), upper)
    joined.append(join((mine.astype(F32) + parts[1]).astype(BF), (parts[2] + parts[3]).astype(BF), 1))
    coef = cols(coef, 1) - dot(joined[1], update_1)
    coef, direct, hot = lax.optimization_barrier((coef, direct, hot))

    mine = cols(coef, 0, 1).astype(BF)
    with_prod = cat(mine, prod)
    got = {1: swap(mine, 1), 2: swap(mine, 2), 3: swap(with_prod, 3)}
    total = mine.astype(F32)
    for mask in (1, 2, 3):
        total = total + cols(got[mask], 0, 1).astype(F32)
    total = total.astype(BF)
    got_prod = cols(got[3], 1)
    siblings.append(cols(got_prod, 0, 1))
    prod = cols(prod, 1) + cols(got_prod, 1).astype(F32)
    got = swap(cat(total, prod), 4)
    got_total, got_prod = cols(got, 0, 1), cols(got, 1)
    joined.append(join(total, got_total, 2))
    siblings.append(cols(got_prod, 0, 1))
    prod = cols(prod, 1) + cols(got_prod, 1).astype(F32)
    coef = cols(coef, 1) - dot(joined[2], update_2)

    sent = cat(coef, pieces)
    got = {mask: swap(sent, mask) for mask in (1, 2, 3)}
    got[0] = sent
    lead = LEVELS - SUMMED
    total = sum(cols(got[mask], 0, lead).astype(F32) for mask in range(4))
    quarters = by_sub([cols(got[mask], lead) for mask in range(4)])
    sent = cat(total, *quarters)
    got = swap(sent, 4)
    total = total + cols(got, 0, lead).astype(F32)
    whole = whole_of(cols(sent, lead), cols(got, lead))
    updates_of = {3: cols(whole, 0, 4), 4: cols(whole, 4, 7)}

    def exchange(level, mask, sent, total, prod):
        left_over = LEVELS - level
        got = swap(sent, mask)
        got_total, got_prod = cols(got, 0, left_over), cols(got, left_over)
        joined.append(join(cols(sent, 0, 1), cols(got_total, 0, 1), level))
        siblings.append(cols(got_prod, 0, 1))
        prod = cols(prod, 1) + cols(got_prod, 1).astype(F32)
        return cols(total, 1) + cols(got_total, 1).astype(F32), prod

    def apply(level, total):
        return total - dot(joined[level], updates_of[level])

    sent = cat(total, prod)
    moved = pl.pallas_call(
        moved_kernel,
        out_shape=shape(points, (LEVELS - BEFORE) * LANE),
        in_specs=[SMEM, VMEM, HBM],
        out_specs=VMEM,
        scratch_shapes=[
            pltpu.VMEM((points, (LEVELS - BEFORE) * LANE), BF),
            pltpu.SemaphoreType.DMA((LEVELS - BEFORE,)),
        ],
        compiler_params=params(12),
        cost_estimate=pl.CostEstimate(flops=1_500_000_000, bytes_accessed=2_000_000, transcendentals=0),
        name="moved",
    )(after(live_counts, sent), hot, left_basis)
    late = after(cols(whole, 7), sent)
    late = late.astype(F32) + swap(late, 32).astype(F32)
    updates_of[5] = cols(late, 0, 2).astype(BF)
    total, prod = exchange(3, 8, sent, total, prod)
    total = apply(3, total)
    total, moved = lax.optimization_barrier((total, moved))

    sent = cat(total, prod)
    late = after(cols(late, 2).astype(BF), sent)
    late = (late.astype(F32) + swap(late, 64).astype(F32)).astype(BF)
    total, prod = exchange(4, 24, sent, total, prod)
    total = apply(4, total)

    total, prod = exchange(5, 32, cat(total, prod), total, prod)
    total = apply(5, total)
    total, updates_of[6] = lax.optimization_barrier((total, late))

    part_prod, part_sol, last_coupling = pl.pallas_call(
        partial_kernel,
        out_shape=(shape(nvec, points, F32),) * 2 + (shape((LEVELS - BEFORE) * 2 * LANE, LANE),),
        in_specs=[SMEM, SMEM, VMEM, HBM] + [VMEM] * (3 + 2 * BEFORE),
        out_specs=(VMEM,) * 3,
        scratch_shapes=[
            pltpu.VMEM((points, BEFORE * LANE), BF),
            pltpu.SemaphoreType.DMA((BEFORE,)),
        ],
        compiler_params=params(12),
        cost_estimate=pl.CostEstimate(flops=2_000_000_000, bytes_accessed=3_000_000, transcendentals=0),
        name="partial",
    )(live_counts, index_1, coupling, left_basis, tree, direct, hot, *siblings, *joined)
    total, prod = exchange(6, 64, cat(total, prod), total, prod)
    total = apply(6, total)
    total, part_prod, part_sol = lax.optimization_barrier((total, part_prod, part_sol))

    exchange(7, 192, cat(total, prod), total, prod)
    return pl.pallas_call(
        last_kernel,
        out_shape=(shape(nvec, points, F32),) * 2,
        in_specs=[VMEM] * (4 + 2 * (LEVELS - BEFORE)),
        out_specs=(VMEM, VMEM),
        compiler_params=params(8),
        cost_estimate=pl.CostEstimate(flops=30_000_000, bytes_accessed=1_000_000, transcendentals=0),
        name="last",
    )(last_coupling, moved, part_prod, part_sol, *siblings[BEFORE:], *joined[BEFORE:])


def solution(mesh):
    placed = (
        P(None, ("leaf", "sub")),
        P(None, ("leaf", "sub")),
        P(("leaf", "sub"), None),
        P(("leaf", "sub")),
        P(("leaf", "sub"), None),
        P(None, ("leaf", "sub"), None),
        P(None, ("leaf", "sub"), None),
        P(("leaf", "sub"), None, None, None),
    )
    return jax.shard_map(
        per_device,
        mesh=mesh,
        in_specs=placed,
        out_specs=(P(None, ("leaf", "sub")), P(None, ("leaf", "sub"))),
        check_vma=False,
    )
```

```python
import functools

import jax
import jax.numpy as jnp
from jax import lax
from jax.experimental import pallas as pl
from jax.experimental.pallas import tpu as pltpu
from jax.sharding import PartitionSpec as P

BF = jnp.bfloat16
F32 = jnp.float32
LANE = 128
VMEM = pl.BlockSpec(memory_space=pltpu.VMEM)
SMEM = pl.BlockSpec(memory_space=pltpu.SMEM)
HBM = pl.BlockSpec(memory_space=pltpu.HBM)
NT = (((1,), (1,)), ((), ()))
LEVELS = 8
SUMMED = 2
BEFORE = 6


def scale(level):
    return 2.0 ** (-0.5 * level)


def dot(a, b):
    return jnp.dot(a, b, preferred_element_type=F32)


def dot_t(a, b):
    return lax.dot_general(a, b, NT, preferred_element_type=F32)


def one_hot(order, low, width):
    rows = lax.broadcasted_iota(jnp.int32, (order.shape[1], width), 0)
    return jnp.where(rows == order[:, low : low + width], 1.0, 0.0).astype(BF)


def columns(ref, level):
    return ref.at[:, pl.ds(level * LANE, LANE)]


def pair_of(ref, level):
    return jnp.concatenate([ref[level], ref[level + 1]], axis=1)


def update_kernel(live, index, order, vec, rhs, coupling, left, right, *rest):
    outs, scratch = rest[: SUMMED + 5], rest[SUMMED + 5 :]
    home, away, bits, tree, right_in = outs[SUMMED:]
    order_in, fields, held, left_in, turned, sems = scratch
    nvec, points = vec.shape
    small = [
        pltpu.make_async_copy(order, order_in, sems.at[0, LEVELS]),
        pltpu.make_async_copy(vec, fields.at[pl.ds(0, nvec)], sems.at[0, LEVELS + 1]),
        pltpu.make_async_copy(rhs, fields.at[pl.ds(nvec, nvec)], sems.at[0, LEVELS + 2]),
    ]
    rights = [pltpu.make_async_copy(right.at[level], right_in.at[level], sems.at[0, level]) for level in range(LEVELS)]
    lefts = [pltpu.make_async_copy(left.at[level], left_in.at[level], sems.at[1, level]) for level in range(LEVELS - 1)]
    coupling_copy = pltpu.make_async_copy(coupling, held, sems.at[1, LEVELS])
    for copy in small + rights[1:] + [coupling_copy] + lefts + rights[:1]:
        copy.start()
    levels = lax.broadcasted_iota(jnp.int32, bits.shape, 0)
    bits[...] = (lax.shift_right_logical(jnp.full(bits.shape, index[0], jnp.int32), levels) & 1).astype(F32)
    for copy in small:
        copy.wait()
    chunk = 256
    for low in range(0, points, chunk):
        moved = dot(fields[...], one_hot(order_in[...], low, chunk))
        slot = lax.broadcasted_iota(jnp.int32, moved.shape, 1) + low
        tree[:, low : low + chunk] = jnp.where(slot < live[0], moved, 0.0).astype(BF)
    for level in range(1, LEVELS):
        rights[level].wait()
        turned[(level - 1) * LANE : level * LANE, :] = right_in[level].T
    coupling_copy.wait()
    second_core = (lax.shift_right_logical(index[0], 2) & 1) == 1
    for low in range(0, LEVELS - 1, 2):
        levels = [level for level in (low, low + 1) if level < LEVELS - 1]
        for level in levels:
            lefts[level].wait()
        block = pair_of(left_in, low) if len(levels) == 2 else left_in[low]
        gram = dot(turned[low * LANE :, :], masked_rows(block, live))
        for level in levels:
            side = slice((level - low) * LANE, (level - low + 1) * LANE)
            own = jnp.concatenate(
                [
                    (gram[(now - low - 1) * LANE : (now - low) * LANE, side] * scale(now)).astype(BF)
                    for now in range(level + 1, LEVELS)
                ],
                axis=0,
            )
            update = dot_t(canonical(held, index, level), own).astype(BF)
            if level < SUMMED:
                outs[level][...] = update
            else:
                at = sum(LEVELS - 1 - below for below in range(SUMMED, level)) * LANE
                to = slice(at, at + update.shape[1])
                first, second = update[:LANE], update[LANE:]
                home[:, to] = jnp.where(second_core, second, first)
                away[:, to] = jnp.where(second_core, first, second)
    rights[0].wait()


def coefficient_kernel(tree, right, first_out, solve_out):
    nvec = first_out.shape[0]
    for level in range(0, LEVELS, 2):
        pair = dot(tree[...], pair_of(right, level))
        for now in (level, level + 1):
            part = pair[:, (now - level) * LANE : (now - level + 1) * LANE] * scale(now)
            first_out[:, (now + 1) * LANE : (now + 2) * LANE] = part[:nvec].astype(BF)
            if now == 0:
                first_out[:, :LANE] = part[nvec:].astype(BF)
            else:
                solve_out[:, (now - 1) * LANE : now * LANE] = part[nvec:]


def canonical(coupling, index, level):
    held = coupling[level]
    swapped = jnp.concatenate([held[LANE:], held[:LANE]], axis=0)
    second = (lax.shift_right_logical(index[0], level) & 1) == 1
    return jnp.where(second, swapped, held)


def direct_kernel(order, tree, block, lead, prod_out, hot_out):
    points = order.shape[1]
    nvec = prod_out.shape[0]
    chunk = 256
    for low in range(0, points, chunk):
        hot_out[:, low : low + chunk] = one_hot(order[...], low, chunk)
    prod_out[...] = dot_t(tree[:nvec, :], block[...])


def masked_rows(block, live):
    rows = lax.broadcasted_iota(jnp.int32, block.shape, 0)
    return jnp.where(rows < live[0], block.astype(F32), 0.0).astype(BF)


def moved_kernel(live, hot, left, moved_out, left_cat, sems):
    copies = [
        pltpu.make_async_copy(left.at[level], columns(left_cat, level - BEFORE), sems.at[level - BEFORE])
        for level in range(BEFORE, LEVELS)
    ]
    for copy in copies:
        copy.start()
    for copy in copies:
        copy.wait()
    moved_out[...] = dot(hot[...], masked_rows(left_cat[...], live)).astype(BF)


def partial_kernel(live, index, coupling, left, tree, direct, hot, *rest):
    siblings, joined = rest[:BEFORE], rest[BEFORE : 2 * BEFORE]
    prod_out, sol_out, coupling_out, left_cat, sems = rest[2 * BEFORE :]
    copies = [
        pltpu.make_async_copy(left.at[level], columns(left_cat, level), sems.at[level])
        for level in range(BEFORE)
    ]
    for copy in copies:
        copy.start()
    for level in range(BEFORE, LEVELS):
        at = (level - BEFORE) * 2 * LANE
        coupling_out[at : at + 2 * LANE, :] = canonical(coupling, index, level)
    coupled = [dot(joined[level][...], canonical(coupling, index, level)).astype(BF) for level in range(BEFORE)]
    siblings = [block[...] for block in siblings]
    terms = jnp.concatenate([jnp.concatenate(siblings, axis=1), jnp.concatenate(coupled, axis=1)], axis=0)
    for copy in copies:
        copy.wait()
    terms = dot_t(terms, left_cat[...])
    nvec = direct.shape[0]
    total = jnp.concatenate([direct[...] + terms[:nvec], tree[nvec:, :].astype(F32) - terms[nvec:]], axis=0)
    slot = lax.broadcasted_iota(jnp.int32, total.shape, 1)
    total = jnp.where(slot < live[0], total, 0.0)
    high = total.astype(BF)
    low = (total - high.astype(F32)).astype(BF)
    both = dot_t(jnp.concatenate([high, low], axis=0), hot[...])
    prod_out[...] = both[:nvec] + both[2 * nvec : 3 * nvec]
    sol_out[...] = both[nvec : 2 * nvec] + both[3 * nvec :]


def last_kernel(coupling, moved, prod, sol, *rest):
    count = LEVELS - BEFORE
    siblings, joined, (prod_out, sol_out) = rest[:count], rest[count : 2 * count], rest[2 * count :]
    coupled = [
        dot(joined[at][...], coupling[2 * at * LANE : 2 * (at + 1) * LANE, :]).astype(BF) for at in range(count)
    ]
    siblings = [block[...] for block in siblings]
    terms = jnp.concatenate([jnp.concatenate(siblings, axis=1), jnp.concatenate(coupled, axis=1)], axis=0)
    terms = dot_t(terms, moved[...])
    nvec = prod.shape[0]
    prod_out[...] = prod[...] + terms[:nvec]
    sol_out[...] = sol[...] - terms[nvec:]


def params(mib):
    return pltpu.CompilerParams(vmem_limit_bytes=mib << 20)


def shape(rows, lanes, dtype=BF):
    return jax.ShapeDtypeStruct((rows, lanes), dtype)


def swap(block, mask):
    count = lax.axis_size("leaf") * lax.axis_size("sub")
    return lax.ppermute(block, ("leaf", "sub"), [(i, i ^ mask) for i in range(count)])


def cols(block, low, high=None):
    return block[:, low * LANE : None if high is None else high * LANE]


def cat(*blocks):
    return jnp.concatenate([block.astype(BF) for block in blocks], axis=1)


def in_hbm(block):
    return pltpu.with_memory_space_constraint(block, pltpu.HBM)


def behind(block, lead):
    def kernel(block_in, lead_in, block_out):
        block_out[...] = block_in[...]

    return pl.pallas_call(
        kernel,
        out_shape=pltpu.VMEM(block.shape, block.dtype),
        in_specs=[VMEM, pl.BlockSpec(memory_space=pl.ANY)],
        out_specs=VMEM,
        compiler_params=params(4),
        cost_estimate=pl.CostEstimate(flops=1_000_000, bytes_accessed=200_000, transcendentals=0),
        name="behind",
    )(block, lead)


def per_device(vectors, right_side, tree_order, live_counts, leaf_block, left_basis, right_bases, coupling):
    nvec, points = vectors.shape
    index = lax.axis_index("leaf") * lax.axis_size("sub") + lax.axis_index("sub")
    index_1 = index.astype(jnp.int32).reshape(1)
    coupling = coupling[0]

    def pick(level, if_set, if_clear):
        side = jnp.broadcast_to(bits[level : level + 1, : if_set.shape[1]], if_set.shape)
        return jnp.where(side > 0, if_set, if_clear)

    def join(mine, other, level):
        return cat(pick(level, other, mine), pick(level, mine, other))

    def whole_of(mine, theirs):
        width = mine.shape[1] // 4
        mine, theirs = (
            jnp.concatenate([half[:, at : at + width] for at in range(0, 4 * width, width)], axis=0)
            for half in (mine, theirs)
        )
        return jnp.concatenate([pick(2, theirs, mine), pick(2, mine, theirs)], axis=0)

    def by_sub(blocks):
        even = [pick(0, blocks[i ^ 1], blocks[i]) for i in range(4)]
        return [pick(1, even[i ^ 2], even[i]) for i in range(4)]

    widths = [LEVELS - 1 - level for level in range(SUMMED)]
    summed = sum(LEVELS - 1 - level for level in range(SUMMED, LEVELS - 1))
    update_0, update_1, home, away, bits, tree, right_in = pl.pallas_call(
        update_kernel,
        out_shape=tuple(pltpu.VMEM((2 * LANE, width * LANE), BF) for width in widths)
        + (pltpu.VMEM((LANE, summed * LANE), BF),) * 2
        + (pltpu.VMEM((LEVELS, 2 * points), F32), pltpu.VMEM((2 * nvec, points), BF))
        + (pltpu.VMEM(right_bases.shape, BF),),
        in_specs=[SMEM, SMEM] + [HBM] * 6,
        out_specs=(VMEM,) * 7,
        scratch_shapes=[
            pltpu.VMEM((1, points), jnp.int32),
            pltpu.VMEM((2 * nvec, points), BF),
            pltpu.VMEM(coupling.shape, BF),
            pltpu.VMEM((LEVELS - 1, points, LANE), BF),
            pltpu.VMEM((7 * LANE, points), BF),
            pltpu.SemaphoreType.DMA((2, LEVELS + 3)),
        ],
        compiler_params=params(20),
        cost_estimate=pl.CostEstimate(flops=1_500_000_000, bytes_accessed=5_000_000, transcendentals=0),
        name="updates",
    )(
        live_counts,
        index_1,
        *map(in_hbm, (tree_order, vectors, right_side, coupling, left_basis, right_bases)),
    )
    got = swap(away, 4)
    first, coef = pl.pallas_call(
        coefficient_kernel,
        out_shape=(pltpu.VMEM((nvec, 9 * LANE), BF), pltpu.VMEM((nvec, 7 * LANE), F32)),
        in_specs=[VMEM, VMEM],
        out_specs=(VMEM, VMEM),
        compiler_params=params(12),
        cost_estimate=pl.CostEstimate(flops=150_000_000, bytes_accessed=2_500_000, transcendentals=0),
        name="coefficients",
    )(tree, right_in)
    halves = (home.astype(F32) + got.astype(F32)).astype(BF)
    piece = halves.shape[0] // 4
    rows_of = by_sub([halves[i * piece : (i + 1) * piece] for i in range(4)])

    siblings, joined = [], []

    sent = {1: cat(first, rows_of[1]), 2: rows_of[2], 3: rows_of[3]}
    got = {mask: swap(sent[mask], mask) for mask in (1, 2, 3)}
    pieces = sum(
        block.astype(F32) for block in (rows_of[0], cols(got[1], 1 + LEVELS), got[2], got[3])
    ).astype(BF)
    joined.append(join(cols(first, 0, 1), cols(got[1], 0, 1), 0))
    siblings.append(cols(got[1], 1, 2))
    prod = cols(first, 2).astype(F32) + cols(got[1], 2, 1 + LEVELS).astype(F32)
    coef = coef - dot(joined[0], update_0)

    mine = cols(coef, 0, 1).astype(BF)
    got = {1: swap(mine, 1), 2: swap(mine, 2), 3: swap(cat(mine, prod), 3)}
    at = [sum(LEVELS - 1 - below for below in range(SUMMED, level)) for level in range(LEVELS)]
    upper = cols(pieces, at[3])
    pieces = cat(cols(pieces, 0, at[3]), upper.astype(F32) + swap(upper, 8).astype(F32))
    parts = {mask: cols(block, 0, 1).astype(F32) for mask, block in got.items()}
    joined.append(join((mine.astype(F32) + parts[1]).astype(BF), (parts[2] + parts[3]).astype(BF), 1))
    got_prod = cols(got[3], 1)
    siblings.append(cols(got_prod, 0, 1))
    prod = cols(prod, 1) + cols(got_prod, 1).astype(F32)
    coef = cols(coef, 1) - dot(joined[1], update_1)

    sent = cat(coef, pieces)
    direct, hot = pl.pallas_call(
        direct_kernel,
        out_shape=(pltpu.VMEM((nvec, points), F32), pltpu.VMEM((points, points), BF)),
        in_specs=[VMEM, VMEM, VMEM, pl.BlockSpec(memory_space=pl.ANY)],
        out_specs=(VMEM, VMEM),
        compiler_params=params(12),
        cost_estimate=pl.CostEstimate(flops=2_000_000_000, bytes_accessed=2_000_000, transcendentals=0),
        name="direct",
    )(tree_order, tree, leaf_block, sent)
    moved = pl.pallas_call(
        moved_kernel,
        out_shape=pltpu.VMEM((points, (LEVELS - BEFORE) * LANE), BF),
        in_specs=[SMEM, VMEM, HBM],
        out_specs=VMEM,
        scratch_shapes=[
            pltpu.VMEM((points, (LEVELS - BEFORE) * LANE), BF),
            pltpu.SemaphoreType.DMA((LEVELS - BEFORE,)),
        ],
        compiler_params=params(12),
        cost_estimate=pl.CostEstimate(flops=1_500_000_000, bytes_accessed=2_000_000, transcendentals=0),
        name="moved",
    )(live_counts, hot, left_basis)
    got = {mask: swap(sent, mask) for mask in (1, 2, 3)}
    got[0] = sent
    lead = LEVELS - SUMMED
    total = sum(cols(got[mask], 0, lead).astype(F32) for mask in range(4))
    quarters = by_sub([cols(got[mask], lead) for mask in range(4)])
    total, moved, direct = lax.optimization_barrier((total, moved, direct))

    early = [cols(quarter, 0, at[4]) for quarter in quarters]
    sent = cat(total, prod, *early)
    late = cat(*(cols(quarter, at[4]) for quarter in quarters))

    def from_four(block, low, high):
        width = block.shape[1] // (4 * LANE)
        return cat(*(cols(block, i * width + low, i * width + high) for i in range(4)))

    def exchange(level, mask, sent, total, prod):
        left_over = LEVELS - level
        got = swap(sent, mask)
        got_total, got_prod = cols(got, 0, left_over), cols(got, left_over, 2 * left_over)
        joined.append(join(cols(sent, 0, 1), cols(got_total, 0, 1), level))
        siblings.append(cols(got_prod, 0, 1))
        prod = cols(prod, 1) + cols(got_prod, 1).astype(F32)
        return cols(total, 1) + cols(got_total, 1).astype(F32), prod, cols(got, 2 * left_over)

    def apply(level, total):
        return total - dot(joined[level], updates_of[level])

    total, prod, theirs = exchange(2, 4, sent, total, prod)
    whole = whole_of(cat(*early), theirs)
    updates_of = {level: cols(whole, at[level], at[level + 1]) for level in (2, 3)}
    total = apply(2, total)

    sent = cat(total, prod)
    late = behind(late, sent)
    late = (late.astype(F32) + swap(late, 24).astype(F32)).astype(BF)
    total, prod, _ = exchange(3, 8, sent, total, prod)
    total = apply(3, total)

    sent = cat(total, prod)
    late = behind(late, sent)
    own, late = from_four(late, 0, 3), from_four(late, 3, 6)
    updates_of[4] = whole_of(own, swap(own, 4))
    late = (late.astype(F32) + swap(late, 32).astype(F32)).astype(BF)
    total, prod, _ = exchange(4, 24, sent, total, prod)
    total = apply(4, total)

    sent = cat(total, prod)
    late = behind(late, sent)
    whole = whole_of(late, swap(late, 4))
    updates_of[5], update_6 = cols(whole, 0, 2), cols(whole, 2)
    total, prod, _ = exchange(5, 32, sent, total, prod)
    total = apply(5, total)

    part_prod, part_sol, last_coupling = pl.pallas_call(
        partial_kernel,
        out_shape=(pltpu.VMEM((nvec, points), F32),) * 2
        + (pltpu.VMEM(((LEVELS - BEFORE) * 2 * LANE, LANE), BF),),
        in_specs=[SMEM, SMEM, VMEM, HBM] + [VMEM] * (3 + 2 * BEFORE),
        out_specs=(VMEM,) * 3,
        scratch_shapes=[
            pltpu.VMEM((points, BEFORE * LANE), BF),
            pltpu.SemaphoreType.DMA((BEFORE,)),
        ],
        compiler_params=params(12),
        cost_estimate=pl.CostEstimate(flops=2_000_000_000, bytes_accessed=3_000_000, transcendentals=0),
        name="partial",
    )(live_counts, index_1, coupling, left_basis, tree, direct, hot, *siblings, *joined)
    rows = [update_6[low : low + nvec] for low in range(0, 2 * LANE, nvec)]
    total, prod, theirs = exchange(6, 64, cat(total, prod, *rows), total, prod)
    theirs = jnp.concatenate([cols(theirs, low, low + 1) for low in range(len(rows))], axis=0)
    updates_of[6] = (update_6.astype(F32) + theirs.astype(F32)).astype(BF)
    total = apply(6, total)
    total, part_prod, part_sol = lax.optimization_barrier((total, part_prod, part_sol))

    exchange(7, 192, cat(total, prod), total, prod)
    return pl.pallas_call(
        last_kernel,
        out_shape=(shape(nvec, points, F32),) * 2,
        in_specs=[VMEM] * (4 + 2 * (LEVELS - BEFORE)),
        out_specs=(VMEM, VMEM),
        compiler_params=params(8),
        cost_estimate=pl.CostEstimate(flops=30_000_000, bytes_accessed=1_000_000, transcendentals=0),
        name="last",
    )(last_coupling, moved, part_prod, part_sol, *siblings[BEFORE:], *joined[BEFORE:])


def solution(mesh):
    placed = (
        P(None, ("leaf", "sub")),
        P(None, ("leaf", "sub")),
        P(("leaf", "sub"), None),
        P(("leaf", "sub")),
        P(("leaf", "sub"), None),
        P(None, ("leaf", "sub"), None),
        P(None, ("leaf", "sub"), None),
        P(("leaf", "sub"), None, None, None),
    )
    return jax.shard_map(
        per_device,
        mesh=mesh,
        in_specs=placed,
        out_specs=(P(None, ("leaf", "sub")), P(None, ("leaf", "sub"))),
        check_vma=False,
    )
```

```python
import functools

import jax
import jax.numpy as jnp
from jax import lax
from jax.experimental import pallas as pl
from jax.experimental.pallas import tpu as pltpu
from jax.sharding import PartitionSpec as P

BF = jnp.bfloat16
F32 = jnp.float32
LANE = 128
VMEM = pl.BlockSpec(memory_space=pltpu.VMEM)
SMEM = pl.BlockSpec(memory_space=pltpu.SMEM)
HBM = pl.BlockSpec(memory_space=pltpu.HBM)
NT = (((1,), (1,)), ((), ()))
LEVELS = 8
SUMMED = 2
BEFORE = 6


def scale(level):
    return 2.0 ** (-0.5 * level)


def dot(a, b):
    return jnp.dot(a, b, preferred_element_type=F32)


def dot_t(a, b):
    return lax.dot_general(a, b, NT, preferred_element_type=F32)


def one_hot(order, low, width):
    rows = lax.broadcasted_iota(jnp.int32, (order.shape[1], width), 0)
    return jnp.where(rows == order[:, low : low + width], 1.0, 0.0).astype(BF)


def columns(ref, level):
    return ref.at[:, pl.ds(level * LANE, LANE)]


def pair_of(ref, level):
    return jnp.concatenate([ref[level], ref[level + 1]], axis=1)


def updates_of_level(gram, low, level, held):
    side = slice((level - low) * LANE, (level - low + 1) * LANE)
    own = jnp.concatenate(
        [
            (gram[(now - low - 1) * LANE : (now - low) * LANE, side] * scale(now)).astype(BF)
            for now in range(level + 1, LEVELS)
        ],
        axis=0,
    )
    return dot_t(held, own).astype(BF)


def summed_kernel(live, index, order, vec, rhs, coupling, left, right, *rest):
    home, away, bits, tree, right_in, turned, order_in, fields, held, left_in, sems = rest
    nvec, points = vec.shape
    small = [
        pltpu.make_async_copy(order, order_in, sems.at[0, LEVELS]),
        pltpu.make_async_copy(vec, fields.at[pl.ds(0, nvec)], sems.at[0, LEVELS + 1]),
        pltpu.make_async_copy(rhs, fields.at[pl.ds(nvec, nvec)], sems.at[0, LEVELS + 2]),
    ]
    rights = [pltpu.make_async_copy(right.at[level], right_in.at[level], sems.at[0, level]) for level in range(LEVELS)]
    lefts = {
        level: pltpu.make_async_copy(left.at[level], left_in.at[level - SUMMED], sems.at[1, level])
        for level in range(SUMMED, LEVELS - 1)
    }
    coupling_copy = pltpu.make_async_copy(coupling, held, sems.at[1, LEVELS])
    for copy in small + [rights[LEVELS - 1]]:
        copy.start()
    coupling_copy.start()
    for level in range(LEVELS - 2, SUMMED - 1, -1):
        lefts[level].start()
        rights[level].start()
    for level in range(SUMMED - 1, -1, -1):
        rights[level].start()
    levels = lax.broadcasted_iota(jnp.int32, bits.shape, 0)
    bits[...] = (lax.shift_right_logical(jnp.full(bits.shape, index[0], jnp.int32), levels) & 1).astype(F32)
    for copy in small:
        copy.wait()
    chunk = 256
    for low in range(0, points, chunk):
        moved = dot(fields[...], one_hot(order_in[...], low, chunk))
        slot = lax.broadcasted_iota(jnp.int32, moved.shape, 1) + low
        tree[:, low : low + chunk] = jnp.where(slot < live[0], moved, 0.0).astype(BF)

    def turn(level):
        rights[level].wait()
        turned[(level - 1) * LANE : level * LANE, :] = right_in[level].T

    turn(LEVELS - 1)
    coupling_copy.wait()
    second_core = (lax.shift_right_logical(index[0], 2) & 1) == 1
    for low in range(LEVELS - 2, SUMMED - 1, -2):
        levels = [level for level in (low, low + 1) if level < LEVELS - 1]
        for level in levels[::-1]:
            lefts[level].wait()
        block = pair_of(left_in, low - SUMMED) if len(levels) == 2 else left_in[low - SUMMED]
        gram = dot(turned[low * LANE :, :], masked_rows(block, live))
        for level in levels:
            update = updates_of_level(gram, low, level, canonical(held, index, level))
            at = sum(LEVELS - 1 - below for below in range(SUMMED, level)) * LANE
            to = slice(at, at + update.shape[1])
            first, second = update[:LANE], update[LANE:]
            home[:, to] = jnp.where(second_core, second, first)
            away[:, to] = jnp.where(second_core, first, second)
        for level in (low, low - 1):
            turn(level)
    rights[0].wait()


def own_kernel(live, index, coupling, left, turned, lead, update_0, update_1, held, left_in, sems):
    copies = [
        pltpu.make_async_copy(coupling.at[pl.ds(0, SUMMED)], held, sems.at[0]),
        pltpu.make_async_copy(left.at[pl.ds(0, SUMMED)], left_in, sems.at[1]),
    ]
    for copy in copies:
        copy.start()
    for copy in copies:
        copy.wait()
    gram = dot(turned[...], masked_rows(pair_of(left_in, 0), live))
    for level, out in ((0, update_0), (1, update_1)):
        out[...] = updates_of_level(gram, 0, level, canonical(held, index, level))


def coefficient_kernel(tree, right, first_out, solve_out):
    nvec = first_out.shape[0]
    for level in range(0, LEVELS, 2):
        pair = dot(tree[...], pair_of(right, level))
        for now in (level, level + 1):
            part = pair[:, (now - level) * LANE : (now - level + 1) * LANE] * scale(now)
            first_out[:, (now + 1) * LANE : (now + 2) * LANE] = part[:nvec].astype(BF)
            if now == 0:
                first_out[:, :LANE] = part[nvec:].astype(BF)
            else:
                solve_out[:, (now - 1) * LANE : now * LANE] = part[nvec:]


def canonical(coupling, index, level):
    held = coupling[level]
    swapped = jnp.concatenate([held[LANE:], held[:LANE]], axis=0)
    second = (lax.shift_right_logical(index[0], level) & 1) == 1
    return jnp.where(second, swapped, held)


def direct_kernel(order, tree, block, lead, prod_out, hot_out):
    points = order.shape[1]
    nvec = prod_out.shape[0]
    chunk = 256
    for low in range(0, points, chunk):
        hot_out[:, low : low + chunk] = one_hot(order[...], low, chunk)
    prod_out[...] = dot_t(tree[:nvec, :], block[...])


def masked_rows(block, live):
    rows = lax.broadcasted_iota(jnp.int32, block.shape, 0)
    return jnp.where(rows < live[0], block.astype(F32), 0.0).astype(BF)


def moved_kernel(live, hot, left, moved_out, left_cat, sems):
    copies = [
        pltpu.make_async_copy(left.at[level], columns(left_cat, level - BEFORE), sems.at[level - BEFORE])
        for level in range(BEFORE, LEVELS)
    ]
    for copy in copies:
        copy.start()
    for copy in copies:
        copy.wait()
    moved_out[...] = dot(hot[...], masked_rows(left_cat[...], live)).astype(BF)


def partial_kernel(live, index, coupling, left, tree, direct, hot, *rest):
    siblings, joined = rest[:BEFORE], rest[BEFORE : 2 * BEFORE]
    prod_out, sol_out, coupling_out, left_cat, sems = rest[2 * BEFORE :]
    copies = [
        pltpu.make_async_copy(left.at[level], columns(left_cat, level), sems.at[level])
        for level in range(BEFORE)
    ]
    for copy in copies:
        copy.start()
    for level in range(BEFORE, LEVELS):
        at = (level - BEFORE) * 2 * LANE
        coupling_out[at : at + 2 * LANE, :] = canonical(coupling, index, level)
    coupled = [dot(joined[level][...], canonical(coupling, index, level)).astype(BF) for level in range(BEFORE)]
    siblings = [block[...] for block in siblings]
    terms = jnp.concatenate([jnp.concatenate(siblings, axis=1), jnp.concatenate(coupled, axis=1)], axis=0)
    for copy in copies:
        copy.wait()
    terms = dot_t(terms, left_cat[...])
    nvec = direct.shape[0]
    total = jnp.concatenate([direct[...] + terms[:nvec], tree[nvec:, :].astype(F32) - terms[nvec:]], axis=0)
    slot = lax.broadcasted_iota(jnp.int32, total.shape, 1)
    total = jnp.where(slot < live[0], total, 0.0)
    high = total.astype(BF)
    low = (total - high.astype(F32)).astype(BF)
    both = dot_t(jnp.concatenate([high, low], axis=0), hot[...])
    prod_out[...] = both[:nvec] + both[2 * nvec : 3 * nvec]
    sol_out[...] = both[nvec : 2 * nvec] + both[3 * nvec :]


def last_kernel(coupling, moved, prod, sol, *rest):
    count = LEVELS - BEFORE
    siblings, joined, (prod_out, sol_out) = rest[:count], rest[count : 2 * count], rest[2 * count :]
    coupled = [
        dot(joined[at][...], coupling[2 * at * LANE : 2 * (at + 1) * LANE, :]).astype(BF) for at in range(count)
    ]
    siblings = [block[...] for block in siblings]
    terms = jnp.concatenate([jnp.concatenate(siblings, axis=1), jnp.concatenate(coupled, axis=1)], axis=0)
    terms = dot_t(terms, moved[...])
    nvec = prod.shape[0]
    prod_out[...] = prod[...] + terms[:nvec]
    sol_out[...] = sol[...] - terms[nvec:]


def params(mib):
    return pltpu.CompilerParams(vmem_limit_bytes=mib << 20)


def shape(rows, lanes, dtype=BF):
    return jax.ShapeDtypeStruct((rows, lanes), dtype)


def swap(block, mask):
    count = lax.axis_size("leaf") * lax.axis_size("sub")
    return lax.ppermute(block, ("leaf", "sub"), [(i, i ^ mask) for i in range(count)])


def cols(block, low, high=None):
    return block[:, low * LANE : None if high is None else high * LANE]


def cat(*blocks):
    return jnp.concatenate([block.astype(BF) for block in blocks], axis=1)


def in_hbm(block):
    return pltpu.with_memory_space_constraint(block, pltpu.HBM)


def behind(lead, *blocks):
    def kernel(lead_in, *refs):
        refs[-1][...] = sum(ref[...].astype(F32) for ref in refs[:-1]).astype(BF)

    return pl.pallas_call(
        kernel,
        out_shape=pltpu.VMEM(blocks[0].shape, BF),
        in_specs=[pl.BlockSpec(memory_space=pl.ANY)] + [VMEM] * len(blocks),
        out_specs=VMEM,
        compiler_params=params(4),
        cost_estimate=pl.CostEstimate(flops=1_000_000, bytes_accessed=200_000, transcendentals=0),
        name="behind",
    )(lead, *blocks)


def per_device(vectors, right_side, tree_order, live_counts, leaf_block, left_basis, right_bases, coupling):
    nvec, points = vectors.shape
    index = lax.axis_index("leaf") * lax.axis_size("sub") + lax.axis_index("sub")
    index_1 = index.astype(jnp.int32).reshape(1)
    coupling = coupling[0]

    def pick(level, if_set, if_clear):
        side = jnp.broadcast_to(bits[level : level + 1, : if_set.shape[1]], if_set.shape)
        return jnp.where(side > 0, if_set, if_clear)

    def join(mine, other, level):
        return cat(pick(level, other, mine), pick(level, mine, other))

    def whole_of(mine, theirs, cost=1):
        width = mine.shape[1] // 4

        def kernel(index_in, mine_in, theirs_in, out):
            second = (lax.shift_right_logical(index_in[0], 2) & 1) == 1
            for at in range(4):
                side = slice(at * width, (at + 1) * width)
                own, other = mine_in[:, side], theirs_in[:, side]
                out[at * nvec : (at + 1) * nvec, :] = jnp.where(second, other, own)
                out[(at + 4) * nvec : (at + 5) * nvec, :] = jnp.where(second, own, other)

        return pl.pallas_call(
            kernel,
            out_shape=pltpu.VMEM((8 * nvec, width), BF),
            in_specs=[SMEM, VMEM, VMEM],
            out_specs=VMEM,
            compiler_params=params(4),
            cost_estimate=pl.CostEstimate(flops=cost * 1_000_000_000, bytes_accessed=1_000_000, transcendentals=0),
            name="whole",
        )(index_1, mine, theirs)

    def by_sub(blocks):
        even = [pick(0, blocks[i ^ 1], blocks[i]) for i in range(4)]
        return [pick(1, even[i ^ 2], even[i]) for i in range(4)]

    summed = sum(LEVELS - 1 - level for level in range(SUMMED, LEVELS - 1))
    home, away, bits, tree, right_in, turned = pl.pallas_call(
        summed_kernel,
        out_shape=(pltpu.VMEM((LANE, summed * LANE), BF),) * 2
        + (pltpu.VMEM((LEVELS, 2 * points), F32), pltpu.VMEM((2 * nvec, points), BF))
        + (pltpu.VMEM(right_bases.shape, BF), pltpu.VMEM((7 * LANE, points), BF)),
        in_specs=[SMEM, SMEM] + [HBM] * 6,
        out_specs=(VMEM,) * 6,
        scratch_shapes=[
            pltpu.VMEM((1, points), jnp.int32),
            pltpu.VMEM((2 * nvec, points), BF),
            pltpu.VMEM(coupling.shape, BF),
            pltpu.VMEM((LEVELS - 1 - SUMMED, points, LANE), BF),
            pltpu.SemaphoreType.DMA((2, LEVELS + 3)),
        ],
        compiler_params=params(20),
        cost_estimate=pl.CostEstimate(flops=1_500_000_000, bytes_accessed=5_000_000, transcendentals=0),
        name="summed",
    )(
        live_counts,
        index_1,
        *map(in_hbm, (tree_order, vectors, right_side, coupling, left_basis, right_bases)),
    )
    got = swap(away, 4)
    first, coef = pl.pallas_call(
        coefficient_kernel,
        out_shape=(pltpu.VMEM((nvec, 9 * LANE), BF), pltpu.VMEM((nvec, 7 * LANE), F32)),
        in_specs=[VMEM, VMEM],
        out_specs=(VMEM, VMEM),
        compiler_params=params(12),
        cost_estimate=pl.CostEstimate(flops=150_000_000, bytes_accessed=2_500_000, transcendentals=0),
        name="coefficients",
    )(tree, right_in)
    halves = (home.astype(F32) + got.astype(F32)).astype(BF)
    piece = halves.shape[0] // 4
    rows_of = by_sub([halves[i * piece : (i + 1) * piece] for i in range(4)])

    siblings, joined = [], []

    sent = {1: cat(first, rows_of[1]), 2: rows_of[2], 3: rows_of[3]}
    update_0, update_1 = pl.pallas_call(
        own_kernel,
        out_shape=(pltpu.VMEM((2 * LANE, 7 * LANE), BF), pltpu.VMEM((2 * LANE, 6 * LANE), BF)),
        in_specs=[SMEM, SMEM, HBM, HBM, VMEM, pl.BlockSpec(memory_space=pl.ANY)],
        out_specs=(VMEM, VMEM),
        scratch_shapes=[
            pltpu.VMEM((SUMMED, 2 * LANE, LANE), BF),
            pltpu.VMEM((SUMMED, points, LANE), BF),
            pltpu.SemaphoreType.DMA((2,)),
        ],
        compiler_params=params(16),
        cost_estimate=pl.CostEstimate(flops=1_500_000_000, bytes_accessed=1_000_000, transcendentals=0),
        name="own",
    )(live_counts, index_1, in_hbm(coupling), in_hbm(left_basis), turned, sent[1])
    got = {mask: swap(sent[mask], mask) for mask in (1, 2, 3)}
    pieces = sum(
        block.astype(F32) for block in (rows_of[0], cols(got[1], 1 + LEVELS), got[2], got[3])
    ).astype(BF)
    joined.append(join(cols(first, 0, 1), cols(got[1], 0, 1), 0))
    siblings.append(cols(got[1], 1, 2))
    prod = cols(first, 2).astype(F32) + cols(got[1], 2, 1 + LEVELS).astype(F32)
    coef = coef - dot(joined[0], update_0)

    mine = cols(coef, 0, 1).astype(BF)
    got = {1: swap(mine, 1), 2: swap(mine, 2), 3: swap(cat(mine, prod), 3)}
    at = [sum(LEVELS - 1 - below for below in range(SUMMED, level)) for level in range(LEVELS)]
    upper = cols(pieces, at[3])
    near = swap(upper, 8)
    far = behind(upper, cols(pieces, at[4]))
    far = swap(far, 16).astype(F32) + swap(far, 24).astype(F32)
    upper = upper.astype(F32) + near.astype(F32)
    pieces = cat(cols(pieces, 0, at[3]), cols(upper, 0, at[4] - at[3]), cols(upper, at[4] - at[3]) + far)
    parts = {mask: cols(block, 0, 1).astype(F32) for mask, block in got.items()}
    joined.append(join((mine.astype(F32) + parts[1]).astype(BF), (parts[2] + parts[3]).astype(BF), 1))
    got_prod = cols(got[3], 1)
    siblings.append(cols(got_prod, 0, 1))
    prod = cols(prod, 1) + cols(got_prod, 1).astype(F32)
    coef = cols(coef, 1) - dot(joined[1], update_1)

    sent = cat(coef, pieces)
    direct, hot = pl.pallas_call(
        direct_kernel,
        out_shape=(pltpu.VMEM((nvec, points), F32), pltpu.VMEM((points, points), BF)),
        in_specs=[VMEM, VMEM, VMEM, pl.BlockSpec(memory_space=pl.ANY)],
        out_specs=(VMEM, VMEM),
        compiler_params=params(12),
        cost_estimate=pl.CostEstimate(flops=2_000_000_000, bytes_accessed=2_000_000, transcendentals=0),
        name="direct",
    )(tree_order, tree, leaf_block, sent)
    moved = pl.pallas_call(
        moved_kernel,
        out_shape=pltpu.VMEM((points, (LEVELS - BEFORE) * LANE), BF),
        in_specs=[SMEM, VMEM, HBM],
        out_specs=VMEM,
        scratch_shapes=[
            pltpu.VMEM((points, (LEVELS - BEFORE) * LANE), BF),
            pltpu.SemaphoreType.DMA((LEVELS - BEFORE,)),
        ],
        compiler_params=params(12),
        cost_estimate=pl.CostEstimate(flops=1_500_000_000, bytes_accessed=2_000_000, transcendentals=0),
        name="moved",
    )(live_counts, hot, left_basis)
    got = {mask: swap(sent, mask) for mask in (1, 2, 3)}
    got[0] = sent
    lead = LEVELS - SUMMED
    total = sum(cols(got[mask], 0, lead).astype(F32) for mask in range(4))
    quarters = by_sub([cols(got[mask], lead) for mask in range(4)])
    total, moved, direct = lax.optimization_barrier((total, moved, direct))

    early = [cols(quarter, 0, at[5]) for quarter in quarters]
    sent = cat(total, prod, *early)
    late = cat(*(cols(quarter, at[5]) for quarter in quarters))

    def from_four(block, low, high):
        width = block.shape[1] // (4 * LANE)
        return cat(*(cols(block, i * width + low, i * width + high) for i in range(4)))

    def exchange(level, mask, sent, total, prod):
        left_over = LEVELS - level
        got = swap(sent, mask)
        got_total, got_prod = cols(got, 0, left_over), cols(got, left_over, 2 * left_over)
        joined.append(join(cols(sent, 0, 1), cols(got_total, 0, 1), level))
        siblings.append(cols(got_prod, 0, 1))
        prod = cols(prod, 1) + cols(got_prod, 1).astype(F32)
        return cols(total, 1) + cols(got_total, 1).astype(F32), prod, cols(got, 2 * left_over)

    def apply(level, total):
        return total - dot(joined[level], updates_of[level])

    total, prod, theirs = exchange(2, 4, sent, total, prod)
    whole = whole_of(cat(*early), theirs)
    updates_of = {level: cols(whole, at[level], at[level + 1]) for level in (2, 3, 4)}
    total = apply(2, total)

    sent = cat(total, prod)
    late = behind(sent, late)
    got_late = swap(late, 32)
    total, prod, _ = exchange(3, 8, sent, total, prod)
    total = apply(3, total)

    sent = cat(total, prod)
    late = behind(sent, late, got_late)
    own, late = from_four(late, 0, 2), from_four(late, 2, 3)
    updates_of[5] = whole_of(own, swap(own, 4))
    got_late = swap(late, 64)
    total, prod, _ = exchange(4, 24, sent, total, prod)
    total = apply(4, total)

    sent = cat(total, prod)
    late = behind(sent, late, got_late)
    updates_of[6] = whole_of(late, swap(late, 4))
    total, prod, _ = exchange(5, 32, sent, total, prod)
    total = apply(5, total)

    part_prod, part_sol, last_coupling = pl.pallas_call(
        partial_kernel,
        out_shape=(pltpu.VMEM((nvec, points), F32),) * 2
        + (pltpu.VMEM(((LEVELS - BEFORE) * 2 * LANE, LANE), BF),),
        in_specs=[SMEM, SMEM, VMEM, HBM] + [VMEM] * (3 + 2 * BEFORE),
        out_specs=(VMEM,) * 3,
        scratch_shapes=[
            pltpu.VMEM((points, BEFORE * LANE), BF),
            pltpu.SemaphoreType.DMA((BEFORE,)),
        ],
        compiler_params=params(12),
        cost_estimate=pl.CostEstimate(flops=2_000_000_000, bytes_accessed=3_000_000, transcendentals=0),
        name="partial",
    )(live_counts, index_1, coupling, left_basis, tree, direct, hot, *siblings, *joined)
    total, prod, _ = exchange(6, 64, cat(total, prod), total, prod)
    total = apply(6, total)
    total, part_prod, part_sol = lax.optimization_barrier((total, part_prod, part_sol))

    exchange(7, 192, cat(total, prod), total, prod)
    return pl.pallas_call(
        last_kernel,
        out_shape=(shape(nvec, points, F32),) * 2,
        in_specs=[VMEM] * (4 + 2 * (LEVELS - BEFORE)),
        out_specs=(VMEM, VMEM),
        compiler_params=params(8),
        cost_estimate=pl.CostEstimate(flops=30_000_000, bytes_accessed=1_000_000, transcendentals=0),
        name="last",
    )(last_coupling, moved, part_prod, part_sol, *siblings[BEFORE:], *joined[BEFORE:])


def solution(mesh):
    placed = (
        P(None, ("leaf", "sub")),
        P(None, ("leaf", "sub")),
        P(("leaf", "sub"), None),
        P(("leaf", "sub")),
        P(("leaf", "sub"), None),
        P(None, ("leaf", "sub"), None),
        P(None, ("leaf", "sub"), None),
        P(("leaf", "sub"), None, None, None),
    )
    return jax.shard_map(
        per_device,
        mesh=mesh,
        in_specs=placed,
        out_specs=(P(None, ("leaf", "sub")), P(None, ("leaf", "sub"))),
        check_vma=False,
    )
```

```python
import functools

import jax
import jax.numpy as jnp
from jax import lax
from jax.experimental import pallas as pl
from jax.experimental.pallas import tpu as pltpu
from jax.sharding import PartitionSpec as P

BF = jnp.bfloat16
F32 = jnp.float32
LANE = 128
VMEM = pl.BlockSpec(memory_space=pltpu.VMEM)
SMEM = pl.BlockSpec(memory_space=pltpu.SMEM)
HBM = pl.BlockSpec(memory_space=pltpu.HBM)
NT = (((1,), (1,)), ((), ()))
LEVELS = 8
SUMMED = 2
BEFORE = 5


def scale(level):
    return 2.0 ** (-0.5 * level)


def dot(a, b):
    return jnp.dot(a, b, preferred_element_type=F32)


def dot_t(a, b):
    return lax.dot_general(a, b, NT, preferred_element_type=F32)


def one_hot(order, low, width):
    rows = lax.broadcasted_iota(jnp.int32, (order.shape[1], width), 0)
    return jnp.where(rows == order[:, low : low + width], 1.0, 0.0).astype(BF)


def columns(ref, level):
    return ref.at[:, pl.ds(level * LANE, LANE)]


def pair_of(ref, level):
    return jnp.concatenate([ref[level], ref[level + 1]], axis=1)


def updates_of_level(gram, low, level, held):
    side = slice((level - low) * LANE, (level - low + 1) * LANE)
    own = jnp.concatenate(
        [
            (gram[(now - low - 1) * LANE : (now - low) * LANE, side] * scale(now)).astype(BF)
            for now in range(level + 1, LEVELS)
        ],
        axis=0,
    )
    return dot_t(held, own).astype(BF)


def summed_kernel(live, index, order, vec, rhs, coupling, left, right, *rest):
    home, away, bits, tree, right_in, turned, order_in, fields, held, left_in, sems = rest
    nvec, points = vec.shape
    small = [
        pltpu.make_async_copy(order, order_in, sems.at[0, LEVELS]),
        pltpu.make_async_copy(vec, fields.at[pl.ds(0, nvec)], sems.at[0, LEVELS + 1]),
        pltpu.make_async_copy(rhs, fields.at[pl.ds(nvec, nvec)], sems.at[0, LEVELS + 2]),
    ]
    rights = [pltpu.make_async_copy(right.at[level], right_in.at[level], sems.at[0, level]) for level in range(LEVELS)]
    lefts = {
        level: pltpu.make_async_copy(left.at[level], left_in.at[level - SUMMED], sems.at[1, level])
        for level in range(SUMMED, LEVELS - 1)
    }
    kept = pl.ds(SUMMED, LEVELS - 1 - SUMMED)
    coupling_copy = pltpu.make_async_copy(coupling.at[kept], held.at[kept], sems.at[1, LEVELS])
    for copy in small + [rights[LEVELS - 1]]:
        copy.start()
    coupling_copy.start()
    for level in range(LEVELS - 2, SUMMED - 1, -1):
        lefts[level].start()
        rights[level].start()
    for level in range(SUMMED - 1, -1, -1):
        rights[level].start()
    levels = lax.broadcasted_iota(jnp.int32, bits.shape, 0)
    bits[...] = (lax.shift_right_logical(jnp.full(bits.shape, index[0], jnp.int32), levels) & 1).astype(F32)
    for copy in small:
        copy.wait()
    chunk = 256
    for low in range(0, points, chunk):
        moved = dot(fields[...], one_hot(order_in[...], low, chunk))
        slot = lax.broadcasted_iota(jnp.int32, moved.shape, 1) + low
        tree[:, low : low + chunk] = jnp.where(slot < live[0], moved, 0.0).astype(BF)

    def turn(level):
        rights[level].wait()
        at = (level - SUMMED - 1) * LANE
        turned[at : at + LANE, :] = right_in[level].T

    turn(LEVELS - 1)
    coupling_copy.wait()
    second_core = (lax.shift_right_logical(index[0], 2) & 1) == 1
    for low in range(LEVELS - 2, SUMMED - 1, -2):
        levels = [level for level in (low, low + 1) if level < LEVELS - 1]
        for level in levels[::-1]:
            lefts[level].wait()
        block = pair_of(left_in, low - SUMMED) if len(levels) == 2 else left_in[low - SUMMED]
        gram = dot(turned[(low - SUMMED) * LANE :, :], masked_rows(block, live))
        for level in levels:
            update = updates_of_level(gram, low, level, canonical(held, index, level))
            at = sum(LEVELS - 1 - below for below in range(SUMMED, level)) * LANE
            to = slice(at, at + update.shape[1])
            first, second = update[:LANE], update[LANE:]
            home[:, to] = jnp.where(second_core, second, first)
            away[:, to] = jnp.where(second_core, first, second)
        if low > SUMMED:
            turn(low)
            turn(low - 1)
    for level in range(SUMMED, -1, -1):
        rights[level].wait()


def own_kernel(live, index, coupling, left, right, turned, lead, update_0, update_1, held, left_in, low_turned, sems):
    copies = [
        pltpu.make_async_copy(coupling.at[pl.ds(0, SUMMED)], held, sems.at[0]),
        pltpu.make_async_copy(left.at[pl.ds(0, SUMMED)], left_in, sems.at[1]),
    ]
    for copy in copies:
        copy.start()
    for level in range(1, SUMMED + 1):
        low_turned[(level - 1) * LANE : level * LANE, :] = right[level].T
    for copy in copies:
        copy.wait()
    block = masked_rows(pair_of(left_in, 0), live)
    gram = jnp.concatenate([dot(low_turned[...], block), dot(turned[...], block)], axis=0)
    for level, out in ((0, update_0), (1, update_1)):
        out[...] = updates_of_level(gram, 0, level, canonical(held, index, level))


def coefficient_kernel(tree, right, first_out, solve_out):
    nvec = first_out.shape[0]
    for level in range(0, LEVELS, 2):
        pair = dot(tree[...], pair_of(right, level))
        for now in (level, level + 1):
            part = pair[:, (now - level) * LANE : (now - level + 1) * LANE] * scale(now)
            first_out[:, (now + 1) * LANE : (now + 2) * LANE] = part[:nvec].astype(BF)
            if now == 0:
                first_out[:, :LANE] = part[nvec:].astype(BF)
            else:
                solve_out[:, (now - 1) * LANE : now * LANE] = part[nvec:]


def canonical(coupling, index, level):
    held = coupling[level]
    swapped = jnp.concatenate([held[LANE:], held[:LANE]], axis=0)
    second = (lax.shift_right_logical(index[0], level) & 1) == 1
    return jnp.where(second, swapped, held)


def direct_kernel(order, tree, block, lead, prod_out, hot_out):
    points = order.shape[1]
    nvec = prod_out.shape[0]
    chunk = 256
    for low in range(0, points, chunk):
        hot_out[:, low : low + chunk] = one_hot(order[...], low, chunk)
    prod_out[...] = dot_t(tree[:nvec, :], block[...])


def masked_rows(block, live):
    rows = lax.broadcasted_iota(jnp.int32, block.shape, 0)
    return jnp.where(rows < live[0], block.astype(F32), 0.0).astype(BF)


def moved_kernel(live, hot, left, moved_out, left_cat, sems):
    copies = [
        pltpu.make_async_copy(left.at[level], columns(left_cat, level - BEFORE), sems.at[level - BEFORE])
        for level in range(BEFORE, LEVELS)
    ]
    for copy in copies:
        copy.start()
    for copy in copies:
        copy.wait()
    moved_out[...] = dot(hot[...], masked_rows(left_cat[...], live)).astype(BF)


def partial_kernel(live, index, coupling, left, tree, direct, hot, *rest):
    siblings, joined = rest[:BEFORE], rest[BEFORE : 2 * BEFORE]
    prod_out, sol_out, coupling_out, left_cat, sems = rest[2 * BEFORE :]
    copies = [
        pltpu.make_async_copy(left.at[level], columns(left_cat, level), sems.at[level])
        for level in range(BEFORE)
    ]
    for copy in copies:
        copy.start()
    for level in range(BEFORE, LEVELS):
        at = (level - BEFORE) * 2 * LANE
        coupling_out[at : at + 2 * LANE, :] = canonical(coupling, index, level)
    coupled = [dot(joined[level][...], canonical(coupling, index, level)).astype(BF) for level in range(BEFORE)]
    siblings = [block[...] for block in siblings]
    terms = jnp.concatenate([jnp.concatenate(siblings, axis=1), jnp.concatenate(coupled, axis=1)], axis=0)
    for copy in copies:
        copy.wait()
    terms = dot_t(terms, left_cat[...])
    nvec = direct.shape[0]
    total = jnp.concatenate([direct[...] + terms[:nvec], tree[nvec:, :].astype(F32) - terms[nvec:]], axis=0)
    slot = lax.broadcasted_iota(jnp.int32, total.shape, 1)
    total = jnp.where(slot < live[0], total, 0.0)
    high = total.astype(BF)
    low = (total - high.astype(F32)).astype(BF)
    both = dot_t(jnp.concatenate([high, low], axis=0), hot[...])
    prod_out[...] = both[:nvec] + both[2 * nvec : 3 * nvec]
    sol_out[...] = both[nvec : 2 * nvec] + both[3 * nvec :]


def last_kernel(coupling, moved, prod, sol, *rest):
    count = LEVELS - BEFORE
    siblings, joined, (prod_out, sol_out) = rest[:count], rest[count : 2 * count], rest[2 * count :]
    coupled = [
        dot(joined[at][...], coupling[2 * at * LANE : 2 * (at + 1) * LANE, :]).astype(BF) for at in range(count)
    ]
    siblings = [block[...] for block in siblings]
    terms = jnp.concatenate([jnp.concatenate(siblings, axis=1), jnp.concatenate(coupled, axis=1)], axis=0)
    terms = dot_t(terms, moved[...])
    nvec = prod.shape[0]
    prod_out[...] = prod[...] + terms[:nvec]
    sol_out[...] = sol[...] - terms[nvec:]


def params(mib):
    return pltpu.CompilerParams(vmem_limit_bytes=mib << 20)


def shape(rows, lanes, dtype=BF):
    return jax.ShapeDtypeStruct((rows, lanes), dtype)


def swap(block, mask):
    count = lax.axis_size("leaf") * lax.axis_size("sub")
    return lax.ppermute(block, ("leaf", "sub"), [(i, i ^ mask) for i in range(count)])


def cols(block, low, high=None):
    return block[:, low * LANE : None if high is None else high * LANE]


def cat(*blocks):
    return jnp.concatenate([block.astype(BF) for block in blocks], axis=1)


def in_hbm(block):
    return pltpu.with_memory_space_constraint(block, pltpu.HBM)


def behind(lead, *blocks):
    def kernel(lead_in, *refs):
        refs[-1][...] = sum(ref[...].astype(F32) for ref in refs[:-1]).astype(BF)

    return pl.pallas_call(
        kernel,
        out_shape=pltpu.VMEM(blocks[0].shape, BF),
        in_specs=[pl.BlockSpec(memory_space=pl.ANY)] + [VMEM] * len(blocks),
        out_specs=VMEM,
        compiler_params=params(4),
        cost_estimate=pl.CostEstimate(flops=1_000_000, bytes_accessed=200_000, transcendentals=0),
        name="behind",
    )(lead, *blocks)


def per_device(vectors, right_side, tree_order, live_counts, leaf_block, left_basis, right_bases, coupling):
    nvec, points = vectors.shape
    index = lax.axis_index("leaf") * lax.axis_size("sub") + lax.axis_index("sub")
    index_1 = index.astype(jnp.int32).reshape(1)
    coupling = coupling[0]

    def pick(level, if_set, if_clear):
        side = jnp.broadcast_to(bits[level : level + 1, : if_set.shape[1]], if_set.shape)
        return jnp.where(side > 0, if_set, if_clear)

    def join(mine, other, level):
        return cat(pick(level, other, mine), pick(level, mine, other))

    def whole_of(mine, theirs, cost=1):
        width = mine.shape[1] // 4

        def kernel(index_in, mine_in, theirs_in, out):
            second = (lax.shift_right_logical(index_in[0], 2) & 1) == 1
            for at in range(4):
                side = slice(at * width, (at + 1) * width)
                own, other = mine_in[:, side], theirs_in[:, side]
                out[at * nvec : (at + 1) * nvec, :] = jnp.where(second, other, own)
                out[(at + 4) * nvec : (at + 5) * nvec, :] = jnp.where(second, own, other)

        return pl.pallas_call(
            kernel,
            out_shape=pltpu.VMEM((8 * nvec, width), BF),
            in_specs=[SMEM, VMEM, VMEM],
            out_specs=VMEM,
            compiler_params=params(4),
            cost_estimate=pl.CostEstimate(flops=cost * 1_000_000_000, bytes_accessed=1_000_000, transcendentals=0),
            name="whole",
        )(index_1, mine, theirs)

    def by_sub(blocks):
        even = [pick(0, blocks[i ^ 1], blocks[i]) for i in range(4)]
        return [pick(1, even[i ^ 2], even[i]) for i in range(4)]

    summed = sum(LEVELS - 1 - level for level in range(SUMMED, LEVELS - 1))
    home, away, bits, tree, right_in, turned = pl.pallas_call(
        summed_kernel,
        out_shape=(pltpu.VMEM((LANE, summed * LANE), BF),) * 2
        + (pltpu.VMEM((LEVELS, 2 * points), F32), pltpu.VMEM((2 * nvec, points), BF))
        + (pltpu.VMEM(right_bases.shape, BF), pltpu.VMEM(((LEVELS - 1 - SUMMED) * LANE, points), BF)),
        in_specs=[SMEM, SMEM] + [HBM] * 6,
        out_specs=(VMEM,) * 6,
        scratch_shapes=[
            pltpu.VMEM((1, points), jnp.int32),
            pltpu.VMEM((2 * nvec, points), BF),
            pltpu.VMEM(coupling.shape, BF),
            pltpu.VMEM((LEVELS - 1 - SUMMED, points, LANE), BF),
            pltpu.SemaphoreType.DMA((2, LEVELS + 3)),
        ],
        compiler_params=params(20),
        cost_estimate=pl.CostEstimate(flops=1_500_000_000, bytes_accessed=5_000_000, transcendentals=0),
        name="summed",
    )(
        live_counts,
        index_1,
        *map(in_hbm, (tree_order, vectors, right_side, coupling, left_basis, right_bases)),
    )
    got = swap(away, 4)
    first, coef = pl.pallas_call(
        coefficient_kernel,
        out_shape=(pltpu.VMEM((nvec, 9 * LANE), BF), pltpu.VMEM((nvec, 7 * LANE), F32)),
        in_specs=[VMEM, VMEM],
        out_specs=(VMEM, VMEM),
        compiler_params=params(12),
        cost_estimate=pl.CostEstimate(flops=150_000_000, bytes_accessed=2_500_000, transcendentals=0),
        name="coefficients",
    )(tree, right_in)
    halves = (home.astype(F32) + got.astype(F32)).astype(BF)
    piece = halves.shape[0] // 4
    rows_of = by_sub([halves[i * piece : (i + 1) * piece] for i in range(4)])

    siblings, joined = [], []

    sent = {1: cat(first, rows_of[1]), 2: rows_of[2], 3: rows_of[3]}
    update_0, update_1 = pl.pallas_call(
        own_kernel,
        out_shape=(pltpu.VMEM((2 * LANE, 7 * LANE), BF), pltpu.VMEM((2 * LANE, 6 * LANE), BF)),
        in_specs=[SMEM, SMEM, HBM, HBM, VMEM, VMEM, pl.BlockSpec(memory_space=pl.ANY)],
        out_specs=(VMEM, VMEM),
        scratch_shapes=[
            pltpu.VMEM((SUMMED, 2 * LANE, LANE), BF),
            pltpu.VMEM((SUMMED, points, LANE), BF),
            pltpu.VMEM((SUMMED * LANE, points), BF),
            pltpu.SemaphoreType.DMA((2,)),
        ],
        compiler_params=params(16),
        cost_estimate=pl.CostEstimate(flops=1_500_000_000, bytes_accessed=1_000_000, transcendentals=0),
        name="own",
    )(live_counts, index_1, in_hbm(coupling), in_hbm(left_basis), right_in, turned, sent[1])
    got = {mask: swap(sent[mask], mask) for mask in (1, 2, 3)}
    pieces = sum(
        block.astype(F32) for block in (rows_of[0], cols(got[1], 1 + LEVELS), got[2], got[3])
    ).astype(BF)
    joined.append(join(cols(first, 0, 1), cols(got[1], 0, 1), 0))
    siblings.append(cols(got[1], 1, 2))
    prod = cols(first, 2).astype(F32) + cols(got[1], 2, 1 + LEVELS).astype(F32)
    coef = coef - dot(joined[0], update_0)

    mine = cols(coef, 0, 1).astype(BF)
    got = {1: swap(mine, 1), 2: swap(mine, 2), 3: swap(cat(mine, prod), 3)}
    at = [sum(LEVELS - 1 - below for below in range(SUMMED, level)) for level in range(LEVELS)]
    upper = cols(pieces, at[3])
    near = swap(upper, 8)
    far = behind(upper, cols(pieces, at[4]))
    far = swap(far, 16).astype(F32) + swap(far, 24).astype(F32)
    upper = upper.astype(F32) + near.astype(F32)
    pieces = cat(cols(pieces, 0, at[3]), cols(upper, 0, at[4] - at[3]), cols(upper, at[4] - at[3]) + far)
    parts = {mask: cols(block, 0, 1).astype(F32) for mask, block in got.items()}
    joined.append(join((mine.astype(F32) + parts[1]).astype(BF), (parts[2] + parts[3]).astype(BF), 1))
    got_prod = cols(got[3], 1)
    siblings.append(cols(got_prod, 0, 1))
    prod = cols(prod, 1) + cols(got_prod, 1).astype(F32)
    coef = cols(coef, 1) - dot(joined[1], update_1)

    sent = cat(coef, pieces)
    direct, hot = pl.pallas_call(
        direct_kernel,
        out_shape=(pltpu.VMEM((nvec, points), F32), pltpu.VMEM((points, points), BF)),
        in_specs=[VMEM, VMEM, VMEM, pl.BlockSpec(memory_space=pl.ANY)],
        out_specs=(VMEM, VMEM),
        compiler_params=params(12),
        cost_estimate=pl.CostEstimate(flops=2_000_000_000, bytes_accessed=2_000_000, transcendentals=0),
        name="direct",
    )(tree_order, tree, leaf_block, sent)
    moved = pl.pallas_call(
        moved_kernel,
        out_shape=pltpu.VMEM((points, (LEVELS - BEFORE) * LANE), BF),
        in_specs=[SMEM, VMEM, HBM],
        out_specs=VMEM,
        scratch_shapes=[
            pltpu.VMEM((points, (LEVELS - BEFORE) * LANE), BF),
            pltpu.SemaphoreType.DMA((LEVELS - BEFORE,)),
        ],
        compiler_params=params(12),
        cost_estimate=pl.CostEstimate(flops=1_500_000_000, bytes_accessed=2_000_000, transcendentals=0),
        name="moved",
    )(live_counts, hot, left_basis)
    got = {mask: swap(sent, mask) for mask in (1, 2, 3)}
    got[0] = sent
    lead = LEVELS - SUMMED
    total = sum(cols(got[mask], 0, lead).astype(F32) for mask in range(4))
    quarters = by_sub([cols(got[mask], lead) for mask in range(4)])
    total, moved, direct = lax.optimization_barrier((total, moved, direct))

    early = [cols(quarter, 0, at[5]) for quarter in quarters]
    sent = cat(total, prod, *early)
    late = cat(*(cols(quarter, at[5]) for quarter in quarters))

    def from_four(block, low, high):
        width = block.shape[1] // (4 * LANE)
        return cat(*(cols(block, i * width + low, i * width + high) for i in range(4)))

    def exchange(level, mask, sent, total, prod):
        left_over = LEVELS - level
        got = swap(sent, mask)
        got_total, got_prod = cols(got, 0, left_over), cols(got, left_over, 2 * left_over)
        joined.append(join(cols(sent, 0, 1), cols(got_total, 0, 1), level))
        siblings.append(cols(got_prod, 0, 1))
        prod = cols(prod, 1) + cols(got_prod, 1).astype(F32)
        return cols(total, 1) + cols(got_total, 1).astype(F32), prod, cols(got, 2 * left_over)

    def apply(level, total):
        return total - dot(joined[level], updates_of[level])

    total, prod, theirs = exchange(2, 4, sent, total, prod)
    whole = whole_of(cat(*early), theirs)
    updates_of = {level: cols(whole, at[level], at[level + 1]) for level in (2, 3, 4)}
    total = apply(2, total)

    sent = cat(total, prod)
    late = behind(sent, late)
    got_late = swap(late, 32)
    total, prod, _ = exchange(3, 8, sent, total, prod)
    total = apply(3, total)

    sent = cat(total, prod)
    late = behind(sent, late, got_late)
    own = from_four(late, 0, 2)
    updates_of[5] = whole_of(own, swap(own, 4))
    got_late = swap(late, 64)
    total, prod, _ = exchange(4, 24, sent, total, prod)
    total = apply(4, total)

    sent = cat(total, prod)
    far = behind(sent, got_late)
    last = from_four(late, 2, 3).astype(F32) + from_four(far, 2, 3).astype(F32)
    own = cat(from_four(far, 0, 2), last)
    theirs = swap(own, 4)
    far_update, updates_of[6] = whole_of(cols(own, 0, 8), cols(theirs, 0, 8)), whole_of(cols(own, 8), cols(theirs, 8))
    part_prod, part_sol, last_coupling = pl.pallas_call(
        partial_kernel,
        out_shape=(pltpu.VMEM((nvec, points), F32),) * 2
        + (pltpu.VMEM(((LEVELS - BEFORE) * 2 * LANE, LANE), BF),),
        in_specs=[SMEM, SMEM, VMEM, HBM] + [VMEM] * (3 + 2 * BEFORE),
        out_specs=(VMEM,) * 3,
        scratch_shapes=[
            pltpu.VMEM((points, BEFORE * LANE), BF),
            pltpu.SemaphoreType.DMA((BEFORE,)),
        ],
        compiler_params=params(12),
        cost_estimate=pl.CostEstimate(flops=2_000_000_000, bytes_accessed=3_000_000, transcendentals=0),
        name="partial",
    )(live_counts, index_1, coupling, left_basis, tree, direct, hot, *siblings, *joined)
    got = [sent] + [swap(sent, mask) for mask in (32, 64, 96)]
    sums = []
    for low, update in ((0, updates_of[5]), (2, far_update)):
        pair = join(cols(got[low], 0, 1), cols(got[low + 1], 0, 1), 5)
        if low == 0:
            joined.append(pair)
        both = [cols(block, 1, 3).astype(F32) for block in got[low : low + 2]]
        sums.append(both[0] + both[1] - dot(pair, update))
    joined.append(join(cols(sums[0], 0, 1).astype(BF), cols(sums[1], 0, 1).astype(BF), 6))
    total = cols(sums[0], 1) + cols(sums[1], 1) - dot(joined[6], updates_of[6])
    siblings.append(cols(got[1], 3, 4))
    siblings.append((cols(got[2], 4, 5).astype(F32) + cols(got[3], 4, 5).astype(F32)).astype(BF))
    prod = sum(cols(block, 5).astype(F32) for block in got)
    total, part_prod, part_sol = lax.optimization_barrier((total, part_prod, part_sol))

    exchange(7, 192, cat(total, prod), total, prod)
    return pl.pallas_call(
        last_kernel,
        out_shape=(shape(nvec, points, F32),) * 2,
        in_specs=[VMEM] * (4 + 2 * (LEVELS - BEFORE)),
        out_specs=(VMEM, VMEM),
        compiler_params=params(8),
        cost_estimate=pl.CostEstimate(flops=30_000_000, bytes_accessed=1_000_000, transcendentals=0),
        name="last",
    )(last_coupling, moved, part_prod, part_sol, *siblings[BEFORE:], *joined[BEFORE:])


def solution(mesh):
    placed = (
        P(None, ("leaf", "sub")),
        P(None, ("leaf", "sub")),
        P(("leaf", "sub"), None),
        P(("leaf", "sub")),
        P(("leaf", "sub"), None),
        P(None, ("leaf", "sub"), None),
        P(None, ("leaf", "sub"), None),
        P(("leaf", "sub"), None, None, None),
    )
    return jax.shard_map(
        per_device,
        mesh=mesh,
        in_specs=placed,
        out_specs=(P(None, ("leaf", "sub")), P(None, ("leaf", "sub"))),
        check_vma=False,
    )
```

```python
import functools

import jax
import jax.numpy as jnp
from jax import lax
from jax.experimental import pallas as pl
from jax.experimental.pallas import tpu as pltpu
from jax.sharding import PartitionSpec as P

BF = jnp.bfloat16
F32 = jnp.float32
LANE = 128
VMEM = pl.BlockSpec(memory_space=pltpu.VMEM)
SMEM = pl.BlockSpec(memory_space=pltpu.SMEM)
HBM = pl.BlockSpec(memory_space=pltpu.HBM)
NT = (((1,), (1,)), ((), ()))
LEVELS = 8
SUMMED = 2
BEFORE = 5


def scale(level):
    return 2.0 ** (-0.5 * level)


def dot(a, b):
    return jnp.dot(a, b, preferred_element_type=F32)


def dot_t(a, b):
    return lax.dot_general(a, b, NT, preferred_element_type=F32)


def one_hot(order, low, width):
    rows = lax.broadcasted_iota(jnp.int32, (order.shape[1], width), 0)
    return jnp.where(rows == order[:, low : low + width], 1.0, 0.0).astype(BF)


def columns(ref, level):
    return ref.at[:, pl.ds(level * LANE, LANE)]


def pair_of(ref, level):
    return jnp.concatenate([ref[level], ref[level + 1]], axis=1)


def updates_of_level(gram, low, level, held):
    side = slice((level - low) * LANE, (level - low + 1) * LANE)
    own = jnp.concatenate(
        [
            (gram[(now - low - 1) * LANE : (now - low) * LANE, side] * scale(now)).astype(BF)
            for now in range(level + 1, LEVELS)
        ],
        axis=0,
    )
    return dot_t(held, own).astype(BF)


def summed_kernel(live, index, order, vec, rhs, coupling, left, right, *rest):
    home, away, bits, order_in, fields, right_in, turned, held, left_in, sems = rest
    nvec, points = vec.shape
    small = [
        pltpu.make_async_copy(order, order_in, sems.at[0, LEVELS]),
        pltpu.make_async_copy(vec, fields.at[pl.ds(0, nvec)], sems.at[0, LEVELS + 1]),
        pltpu.make_async_copy(rhs, fields.at[pl.ds(nvec, nvec)], sems.at[0, LEVELS + 2]),
    ]
    rights = [pltpu.make_async_copy(right.at[level], right_in.at[level], sems.at[0, level]) for level in range(LEVELS)]
    lefts = {
        level: pltpu.make_async_copy(left.at[level], left_in.at[level - SUMMED], sems.at[1, level])
        for level in range(SUMMED, LEVELS - 1)
    }
    kept = pl.ds(SUMMED, LEVELS - 1 - SUMMED)
    coupling_copy = pltpu.make_async_copy(coupling.at[kept], held.at[kept], sems.at[1, LEVELS])
    rights[LEVELS - 1].start()
    coupling_copy.start()
    for level in range(LEVELS - 2, SUMMED - 1, -1):
        lefts[level].start()
        rights[level].start()
    for copy in small + rights[SUMMED - 1 :: -1]:
        copy.start()
    levels = lax.broadcasted_iota(jnp.int32, bits.shape, 0)
    bits[...] = (lax.shift_right_logical(jnp.full(bits.shape, index[0], jnp.int32), levels) & 1).astype(F32)

    def turn(level):
        rights[level].wait()
        at = (level - SUMMED - 1) * LANE
        turned[at : at + LANE, :] = right_in[level].T

    turn(LEVELS - 1)
    coupling_copy.wait()
    second_core = (lax.shift_right_logical(index[0], 2) & 1) == 1
    for low in range(LEVELS - 2, SUMMED - 1, -2):
        levels = [level for level in (low, low + 1) if level < LEVELS - 1]
        for level in levels[::-1]:
            lefts[level].wait()
        block = pair_of(left_in, low - SUMMED) if len(levels) == 2 else left_in[low - SUMMED]
        gram = dot(turned[(low - SUMMED) * LANE :, :], masked_rows(block, live))
        for level in levels:
            update = updates_of_level(gram, low, level, canonical(held, index, level))
            at = sum(LEVELS - 1 - below for below in range(SUMMED, level)) * LANE
            to = slice(at, at + update.shape[1])
            first, second = update[:LANE], update[LANE:]
            home[:, to] = jnp.where(second_core, second, first)
            away[:, to] = jnp.where(second_core, first, second)
        if low > SUMMED:
            turn(low)
            turn(low - 1)
    for copy in rights[SUMMED::-1] + small:
        copy.wait()


def own_kernel(live, index, coupling, left, right, turned, lead, update_0, update_1, held, left_in, low_turned, sems):
    copies = [
        pltpu.make_async_copy(coupling.at[pl.ds(0, SUMMED)], held, sems.at[0]),
        pltpu.make_async_copy(left.at[pl.ds(0, SUMMED)], left_in, sems.at[1]),
    ]
    for copy in copies:
        copy.start()
    for level in range(1, SUMMED + 1):
        low_turned[(level - 1) * LANE : level * LANE, :] = right[level].T
    for copy in copies:
        copy.wait()
    block = masked_rows(pair_of(left_in, 0), live)
    gram = jnp.concatenate([dot(low_turned[...], block), dot(turned[...], block)], axis=0)
    for level, out in ((0, update_0), (1, update_1)):
        out[...] = updates_of_level(gram, 0, level, canonical(held, index, level))


def coefficient_kernel(live, order, fields, right, first_out, solve_out, tree):
    nvec = first_out.shape[0]
    points = order.shape[1]
    chunk = 256
    for low in range(0, points, chunk):
        moved = dot(fields[...], one_hot(order[...], low, chunk))
        slot = lax.broadcasted_iota(jnp.int32, moved.shape, 1) + low
        tree[:, low : low + chunk] = jnp.where(slot < live[0], moved, 0.0).astype(BF)
    for level in range(0, LEVELS, 2):
        pair = dot(tree[...], pair_of(right, level))
        for now in (level, level + 1):
            part = pair[:, (now - level) * LANE : (now - level + 1) * LANE] * scale(now)
            first_out[:, (now + 1) * LANE : (now + 2) * LANE] = part[:nvec].astype(BF)
            if now == 0:
                first_out[:, :LANE] = part[nvec:].astype(BF)
            else:
                solve_out[:, (now - 1) * LANE : now * LANE] = part[nvec:]


def canonical(coupling, index, level):
    held = coupling[level]
    swapped = jnp.concatenate([held[LANE:], held[:LANE]], axis=0)
    second = (lax.shift_right_logical(index[0], level) & 1) == 1
    return jnp.where(second, swapped, held)


def direct_kernel(order, tree, block, lead, prod_out, hot_out):
    points = order.shape[1]
    nvec = prod_out.shape[0]
    chunk = 256
    for low in range(0, points, chunk):
        hot_out[:, low : low + chunk] = one_hot(order[...], low, chunk)
    prod_out[...] = dot_t(tree[:nvec, :], block[...])


def masked_rows(block, live):
    rows = lax.broadcasted_iota(jnp.int32, block.shape, 0)
    return jnp.where(rows < live[0], block.astype(F32), 0.0).astype(BF)


def moved_kernel(live, hot, left, moved_out, left_cat, sems):
    copies = [
        pltpu.make_async_copy(left.at[level], columns(left_cat, level - BEFORE), sems.at[level - BEFORE])
        for level in range(BEFORE, LEVELS)
    ]
    for copy in copies:
        copy.start()
    for copy in copies:
        copy.wait()
    moved_out[...] = dot(hot[...], masked_rows(left_cat[...], live)).astype(BF)


def partial_kernel(live, index, coupling, left, tree, direct, hot, *rest):
    siblings, joined = rest[:BEFORE], rest[BEFORE : 2 * BEFORE]
    prod_out, sol_out, coupling_out, left_cat, sems = rest[2 * BEFORE :]
    copies = [
        pltpu.make_async_copy(left.at[level], columns(left_cat, level), sems.at[level])
        for level in range(BEFORE)
    ]
    for copy in copies:
        copy.start()
    for level in range(BEFORE, LEVELS):
        at = (level - BEFORE) * 2 * LANE
        coupling_out[at : at + 2 * LANE, :] = canonical(coupling, index, level)
    coupled = [dot(joined[level][...], canonical(coupling, index, level)).astype(BF) for level in range(BEFORE)]
    siblings = [block[...] for block in siblings]
    terms = jnp.concatenate([jnp.concatenate(siblings, axis=1), jnp.concatenate(coupled, axis=1)], axis=0)
    for copy in copies:
        copy.wait()
    terms = dot_t(terms, left_cat[...])
    nvec = direct.shape[0]
    total = jnp.concatenate([direct[...] + terms[:nvec], tree[nvec:, :].astype(F32) - terms[nvec:]], axis=0)
    slot = lax.broadcasted_iota(jnp.int32, total.shape, 1)
    total = jnp.where(slot < live[0], total, 0.0)
    high = total.astype(BF)
    low = (total - high.astype(F32)).astype(BF)
    both = dot_t(jnp.concatenate([high, low], axis=0), hot[...])
    prod_out[...] = both[:nvec] + both[2 * nvec : 3 * nvec]
    sol_out[...] = both[nvec : 2 * nvec] + both[3 * nvec :]


def last_kernel(coupling, moved, prod, sol, *rest):
    count = LEVELS - BEFORE
    siblings, joined, (prod_out, sol_out) = rest[:count], rest[count : 2 * count], rest[2 * count :]
    coupled = [
        dot(joined[at][...], coupling[2 * at * LANE : 2 * (at + 1) * LANE, :]).astype(BF) for at in range(count)
    ]
    siblings = [block[...] for block in siblings]
    terms = jnp.concatenate([jnp.concatenate(siblings, axis=1), jnp.concatenate(coupled, axis=1)], axis=0)
    terms = dot_t(terms, moved[...])
    nvec = prod.shape[0]
    prod_out[...] = prod[...] + terms[:nvec]
    sol_out[...] = sol[...] - terms[nvec:]


def params(mib):
    return pltpu.CompilerParams(vmem_limit_bytes=mib << 20)


def shape(rows, lanes, dtype=BF):
    return jax.ShapeDtypeStruct((rows, lanes), dtype)


def swap(block, mask):
    count = lax.axis_size("leaf") * lax.axis_size("sub")
    return lax.ppermute(block, ("leaf", "sub"), [(i, i ^ mask) for i in range(count)])


def cols(block, low, high=None):
    return block[:, low * LANE : None if high is None else high * LANE]


def cat(*blocks):
    return jnp.concatenate([block.astype(BF) for block in blocks], axis=1)


def in_hbm(block):
    return pltpu.with_memory_space_constraint(block, pltpu.HBM)


def behind(lead, *blocks):
    def kernel(lead_in, *refs):
        refs[-1][...] = sum(ref[...].astype(F32) for ref in refs[:-1]).astype(BF)

    return pl.pallas_call(
        kernel,
        out_shape=pltpu.VMEM(blocks[0].shape, BF),
        in_specs=[pl.BlockSpec(memory_space=pl.ANY)] + [VMEM] * len(blocks),
        out_specs=VMEM,
        compiler_params=params(4),
        cost_estimate=pl.CostEstimate(flops=1_000_000, bytes_accessed=200_000, transcendentals=0),
        name="behind",
    )(lead, *blocks)


def per_device(vectors, right_side, tree_order, live_counts, leaf_block, left_basis, right_bases, coupling):
    nvec, points = vectors.shape
    index = lax.axis_index("leaf") * lax.axis_size("sub") + lax.axis_index("sub")
    index_1 = index.astype(jnp.int32).reshape(1)
    coupling = coupling[0]

    def pick(level, if_set, if_clear):
        side = jnp.broadcast_to(bits[level : level + 1, : if_set.shape[1]], if_set.shape)
        return jnp.where(side > 0, if_set, if_clear)

    def join(mine, other, level):
        return cat(pick(level, other, mine), pick(level, mine, other))

    def whole_of(mine, theirs, cost=1):
        width = mine.shape[1] // 4

        def kernel(index_in, mine_in, theirs_in, out):
            second = (lax.shift_right_logical(index_in[0], 2) & 1) == 1
            for at in range(4):
                side = slice(at * width, (at + 1) * width)
                own, other = mine_in[:, side], theirs_in[:, side]
                out[at * nvec : (at + 1) * nvec, :] = jnp.where(second, other, own)
                out[(at + 4) * nvec : (at + 5) * nvec, :] = jnp.where(second, own, other)

        return pl.pallas_call(
            kernel,
            out_shape=pltpu.VMEM((8 * nvec, width), BF),
            in_specs=[SMEM, VMEM, VMEM],
            out_specs=VMEM,
            compiler_params=params(4),
            cost_estimate=pl.CostEstimate(flops=cost * 1_000_000_000, bytes_accessed=1_000_000, transcendentals=0),
            name="whole",
        )(index_1, mine, theirs)

    def by_sub(blocks):
        even = [pick(0, blocks[i ^ 1], blocks[i]) for i in range(4)]
        return [pick(1, even[i ^ 2], even[i]) for i in range(4)]

    summed = sum(LEVELS - 1 - level for level in range(SUMMED, LEVELS - 1))
    home, away, bits, order_in, fields, right_in, turned = pl.pallas_call(
        summed_kernel,
        out_shape=(pltpu.VMEM((LANE, summed * LANE), BF),) * 2
        + (pltpu.VMEM((LEVELS, 2 * points), F32), pltpu.VMEM((1, points), jnp.int32), pltpu.VMEM((2 * nvec, points), BF))
        + (pltpu.VMEM(right_bases.shape, BF), pltpu.VMEM(((LEVELS - 1 - SUMMED) * LANE, points), BF)),
        in_specs=[SMEM, SMEM] + [HBM] * 6,
        out_specs=(VMEM,) * 7,
        scratch_shapes=[
            pltpu.VMEM(coupling.shape, BF),
            pltpu.VMEM((LEVELS - 1 - SUMMED, points, LANE), BF),
            pltpu.SemaphoreType.DMA((2, LEVELS + 3)),
        ],
        compiler_params=params(20),
        cost_estimate=pl.CostEstimate(flops=1_500_000_000, bytes_accessed=5_000_000, transcendentals=0),
        name="summed",
    )(
        live_counts,
        index_1,
        *map(in_hbm, (tree_order, vectors, right_side, coupling, left_basis, right_bases)),
    )
    got = swap(away, 4)
    first, coef, tree = pl.pallas_call(
        coefficient_kernel,
        out_shape=(
            pltpu.VMEM((nvec, 9 * LANE), BF),
            pltpu.VMEM((nvec, 7 * LANE), F32),
            pltpu.VMEM((2 * nvec, points), BF),
        ),
        in_specs=[SMEM, VMEM, VMEM, VMEM],
        out_specs=(VMEM,) * 3,
        compiler_params=params(12),
        cost_estimate=pl.CostEstimate(flops=300_000_000, bytes_accessed=2_500_000, transcendentals=0),
        name="coefficients",
    )(live_counts, order_in, fields, right_in)
    halves = (home.astype(F32) + got.astype(F32)).astype(BF)
    piece = halves.shape[0] // 4
    rows_of = by_sub([halves[i * piece : (i + 1) * piece] for i in range(4)])

    siblings, joined = [], []

    sent = {1: cat(first, rows_of[1]), 2: rows_of[2], 3: rows_of[3]}
    update_0, update_1 = pl.pallas_call(
        own_kernel,
        out_shape=(pltpu.VMEM((2 * LANE, 7 * LANE), BF), pltpu.VMEM((2 * LANE, 6 * LANE), BF)),
        in_specs=[SMEM, SMEM, HBM, HBM, VMEM, VMEM, pl.BlockSpec(memory_space=pl.ANY)],
        out_specs=(VMEM, VMEM),
        scratch_shapes=[
            pltpu.VMEM((SUMMED, 2 * LANE, LANE), BF),
            pltpu.VMEM((SUMMED, points, LANE), BF),
            pltpu.VMEM((SUMMED * LANE, points), BF),
            pltpu.SemaphoreType.DMA((2,)),
        ],
        compiler_params=params(16),
        cost_estimate=pl.CostEstimate(flops=1_500_000_000, bytes_accessed=1_000_000, transcendentals=0),
        name="own",
    )(live_counts, index_1, in_hbm(coupling), in_hbm(left_basis), right_in, turned, sent[1])
    got = {mask: swap(sent[mask], mask) for mask in (1, 2, 3)}
    pieces = sum(
        block.astype(F32) for block in (rows_of[0], cols(got[1], 1 + LEVELS), got[2], got[3])
    ).astype(BF)
    joined.append(join(cols(first, 0, 1), cols(got[1], 0, 1), 0))
    siblings.append(cols(got[1], 1, 2))
    prod = cols(first, 2).astype(F32) + cols(got[1], 2, 1 + LEVELS).astype(F32)
    coef = coef - dot(joined[0], update_0)

    mine = cols(coef, 0, 1).astype(BF)
    got = {1: swap(mine, 1), 2: swap(mine, 2), 3: swap(cat(mine, prod), 3)}
    at = [sum(LEVELS - 1 - below for below in range(SUMMED, level)) for level in range(LEVELS)]
    upper = cols(pieces, at[3])
    near = swap(upper, 8)
    far = behind(upper, cols(pieces, at[4]))
    far = swap(far, 16).astype(F32) + swap(far, 24).astype(F32)
    upper = upper.astype(F32) + near.astype(F32)
    pieces = cat(cols(pieces, 0, at[3]), cols(upper, 0, at[4] - at[3]), cols(upper, at[4] - at[3]) + far)
    parts = {mask: cols(block, 0, 1).astype(F32) for mask, block in got.items()}
    joined.append(join((mine.astype(F32) + parts[1]).astype(BF), (parts[2] + parts[3]).astype(BF), 1))
    got_prod = cols(got[3], 1)
    siblings.append(cols(got_prod, 0, 1))
    prod = cols(prod, 1) + cols(got_prod, 1).astype(F32)
    coef = cols(coef, 1) - dot(joined[1], update_1)

    sent = cat(coef, pieces)
    direct, hot = pl.pallas_call(
        direct_kernel,
        out_shape=(pltpu.VMEM((nvec, points), F32), pltpu.VMEM((points, points), BF)),
        in_specs=[VMEM, VMEM, VMEM, pl.BlockSpec(memory_space=pl.ANY)],
        out_specs=(VMEM, VMEM),
        compiler_params=params(12),
        cost_estimate=pl.CostEstimate(flops=2_000_000_000, bytes_accessed=2_000_000, transcendentals=0),
        name="direct",
    )(tree_order, tree, leaf_block, sent)
    moved = pl.pallas_call(
        moved_kernel,
        out_shape=pltpu.VMEM((points, (LEVELS - BEFORE) * LANE), BF),
        in_specs=[SMEM, VMEM, HBM],
        out_specs=VMEM,
        scratch_shapes=[
            pltpu.VMEM((points, (LEVELS - BEFORE) * LANE), BF),
            pltpu.SemaphoreType.DMA((LEVELS - BEFORE,)),
        ],
        compiler_params=params(12),
        cost_estimate=pl.CostEstimate(flops=1_500_000_000, bytes_accessed=2_000_000, transcendentals=0),
        name="moved",
    )(live_counts, hot, left_basis)
    got = {mask: swap(sent, mask) for mask in (1, 2, 3)}
    got[0] = sent
    lead = LEVELS - SUMMED
    total = sum(cols(got[mask], 0, lead).astype(F32) for mask in range(4))
    quarters = by_sub([cols(got[mask], lead) for mask in range(4)])
    total, moved, direct = lax.optimization_barrier((total, moved, direct))

    early = [cols(quarter, 0, at[5]) for quarter in quarters]
    sent = cat(total, prod, *early)
    late = cat(*(cols(quarter, at[5]) for quarter in quarters))

    def from_four(block, low, high):
        width = block.shape[1] // (4 * LANE)
        return cat(*(cols(block, i * width + low, i * width + high) for i in range(4)))

    def exchange(level, mask, sent, total, prod):
        left_over = LEVELS - level
        got = swap(sent, mask)
        got_total, got_prod = cols(got, 0, left_over), cols(got, left_over, 2 * left_over)
        joined.append(join(cols(sent, 0, 1), cols(got_total, 0, 1), level))
        siblings.append(cols(got_prod, 0, 1))
        prod = cols(prod, 1) + cols(got_prod, 1).astype(F32)
        return cols(total, 1) + cols(got_total, 1).astype(F32), prod, cols(got, 2 * left_over)

    def apply(level, total):
        return total - dot(joined[level], updates_of[level])

    total, prod, theirs = exchange(2, 4, sent, total, prod)
    whole = whole_of(cat(*early), theirs)
    updates_of = {level: cols(whole, at[level], at[level + 1]) for level in (2, 3, 4)}
    total = apply(2, total)

    sent = cat(total, prod)
    late = behind(sent, late)
    got_late = swap(late, 32)
    total, prod, _ = exchange(3, 8, sent, total, prod)
    total = apply(3, total)

    sent = cat(total, prod)
    late = behind(sent, late, got_late)
    own = from_four(late, 0, 2)
    updates_of[5] = whole_of(own, swap(own, 4))
    got_late = swap(late, 64)
    total, prod, _ = exchange(4, 24, sent, total, prod)
    total = apply(4, total)

    sent = cat(total, prod)
    far = behind(sent, got_late)
    last = from_four(late, 2, 3).astype(F32) + from_four(far, 2, 3).astype(F32)
    own = cat(from_four(far, 0, 2), last)
    theirs = swap(own, 4)
    far_update, updates_of[6] = whole_of(cols(own, 0, 8), cols(theirs, 0, 8)), whole_of(cols(own, 8), cols(theirs, 8))
    part_prod, part_sol, last_coupling = pl.pallas_call(
        partial_kernel,
        out_shape=(pltpu.VMEM((nvec, points), F32),) * 2
        + (pltpu.VMEM(((LEVELS - BEFORE) * 2 * LANE, LANE), BF),),
        in_specs=[SMEM, SMEM, VMEM, HBM] + [VMEM] * (3 + 2 * BEFORE),
        out_specs=(VMEM,) * 3,
        scratch_shapes=[
            pltpu.VMEM((points, BEFORE * LANE), BF),
            pltpu.SemaphoreType.DMA((BEFORE,)),
        ],
        compiler_params=params(12),
        cost_estimate=pl.CostEstimate(flops=2_000_000_000, bytes_accessed=3_000_000, transcendentals=0),
        name="partial",
    )(live_counts, index_1, coupling, left_basis, tree, direct, hot, *siblings, *joined)
    got = [sent] + [swap(sent, mask) for mask in (32, 64, 96)]
    sums = []
    for low, update in ((0, updates_of[5]), (2, far_update)):
        pair = join(cols(got[low], 0, 1), cols(got[low + 1], 0, 1), 5)
        if low == 0:
            joined.append(pair)
        both = [cols(block, 1, 3).astype(F32) for block in got[low : low + 2]]
        sums.append(both[0] + both[1] - dot(pair, update))
    joined.append(join(cols(sums[0], 0, 1).astype(BF), cols(sums[1], 0, 1).astype(BF), 6))
    total = cols(sums[0], 1) + cols(sums[1], 1) - dot(joined[6], updates_of[6])
    siblings.append(cols(got[1], 3, 4))
    siblings.append((cols(got[2], 4, 5).astype(F32) + cols(got[3], 4, 5).astype(F32)).astype(BF))
    prod = sum(cols(block, 5).astype(F32) for block in got)
    total, part_prod, part_sol = lax.optimization_barrier((total, part_prod, part_sol))

    exchange(7, 192, cat(total, prod), total, prod)
    return pl.pallas_call(
        last_kernel,
        out_shape=(shape(nvec, points, F32),) * 2,
        in_specs=[VMEM] * (4 + 2 * (LEVELS - BEFORE)),
        out_specs=(VMEM, VMEM),
        compiler_params=params(8),
        cost_estimate=pl.CostEstimate(flops=30_000_000, bytes_accessed=1_000_000, transcendentals=0),
        name="last",
    )(last_coupling, moved, part_prod, part_sol, *siblings[BEFORE:], *joined[BEFORE:])


def solution(mesh):
    placed = (
        P(None, ("leaf", "sub")),
        P(None, ("leaf", "sub")),
        P(("leaf", "sub"), None),
        P(("leaf", "sub")),
        P(("leaf", "sub"), None),
        P(None, ("leaf", "sub"), None),
        P(None, ("leaf", "sub"), None),
        P(("leaf", "sub"), None, None, None),
    )
    return jax.shard_map(
        per_device,
        mesh=mesh,
        in_specs=placed,
        out_specs=(P(None, ("leaf", "sub")), P(None, ("leaf", "sub"))),
        check_vma=False,
    )
```

```python
import functools

import jax
import jax.numpy as jnp
from jax import lax
from jax.experimental import pallas as pl
from jax.experimental.pallas import tpu as pltpu
from jax.sharding import PartitionSpec as P

BF = jnp.bfloat16
F32 = jnp.float32
LANE = 128
VMEM = pl.BlockSpec(memory_space=pltpu.VMEM)
SMEM = pl.BlockSpec(memory_space=pltpu.SMEM)
HBM = pl.BlockSpec(memory_space=pltpu.HBM)
NT = (((1,), (1,)), ((), ()))
LEVELS = 8
SUMMED = 2
BEFORE = 5


def scale(level):
    return 2.0 ** (-0.5 * level)


def dot(a, b):
    return jnp.dot(a, b, preferred_element_type=F32)


def dot_t(a, b):
    return lax.dot_general(a, b, NT, preferred_element_type=F32)


def one_hot(order, low, width):
    rows = lax.broadcasted_iota(jnp.int32, (order.shape[1], width), 0)
    return jnp.where(rows == order[:, low : low + width], 1.0, 0.0).astype(BF)


def columns(ref, level):
    return ref.at[:, pl.ds(level * LANE, LANE)]


def pair_of(ref, level):
    return jnp.concatenate([ref[level], ref[level + 1]], axis=1)


def updates_of_level(gram, low, level, held):
    side = slice((level - low) * LANE, (level - low + 1) * LANE)
    own = jnp.concatenate(
        [
            (gram[(now - low - 1) * LANE : (now - low) * LANE, side] * scale(now)).astype(BF)
            for now in range(level + 1, LEVELS)
        ],
        axis=0,
    )
    return dot_t(held, own).astype(BF)


def summed_kernel(live, index, order, vec, rhs, coupling, left, right, *rest):
    home, away, bits, order_in, fields, right_in, turned, held, left_in, sems = rest
    nvec, points = vec.shape
    small = [
        pltpu.make_async_copy(order, order_in, sems.at[0, LEVELS]),
        pltpu.make_async_copy(vec, fields.at[pl.ds(0, nvec)], sems.at[0, LEVELS + 1]),
        pltpu.make_async_copy(rhs, fields.at[pl.ds(nvec, nvec)], sems.at[0, LEVELS + 2]),
    ]
    rights = [pltpu.make_async_copy(right.at[level], right_in.at[level], sems.at[0, level]) for level in range(LEVELS)]
    lefts = {
        level: pltpu.make_async_copy(left.at[level], left_in.at[level - SUMMED], sems.at[1, level])
        for level in range(SUMMED, LEVELS - 1)
    }
    kept = pl.ds(SUMMED, LEVELS - 1 - SUMMED)
    coupling_copy = pltpu.make_async_copy(coupling.at[kept], held.at[kept], sems.at[1, LEVELS])
    rights[LEVELS - 1].start()
    coupling_copy.start()
    for level in range(LEVELS - 2, SUMMED - 1, -1):
        lefts[level].start()
        rights[level].start()
    for copy in small + rights[SUMMED - 1 :: -1]:
        copy.start()
    levels = lax.broadcasted_iota(jnp.int32, bits.shape, 0)
    bits[...] = (lax.shift_right_logical(jnp.full(bits.shape, index[0], jnp.int32), levels) & 1).astype(F32)

    def turn(level):
        rights[level].wait()
        at = (level - SUMMED - 1) * LANE
        turned[at : at + LANE, :] = right_in[level].T

    turn(LEVELS - 1)
    coupling_copy.wait()
    second_core = (lax.shift_right_logical(index[0], 2) & 1) == 1
    for low in range(LEVELS - 2, SUMMED - 1, -2):
        levels = [level for level in (low, low + 1) if level < LEVELS - 1]
        for level in levels[::-1]:
            lefts[level].wait()
        block = pair_of(left_in, low - SUMMED) if len(levels) == 2 else left_in[low - SUMMED]
        gram = dot(turned[(low - SUMMED) * LANE :, :], masked_rows(block, live))
        for level in levels:
            update = updates_of_level(gram, low, level, canonical(held, index, level))
            at = sum(LEVELS - 1 - below for below in range(SUMMED, level)) * LANE
            to = slice(at, at + update.shape[1])
            first, second = update[:LANE], update[LANE:]
            home[:, to] = jnp.where(second_core, second, first)
            away[:, to] = jnp.where(second_core, first, second)
        if low > SUMMED:
            turn(low)
            turn(low - 1)
    for copy in rights[SUMMED::-1] + small:
        copy.wait()


def own_kernel(live, index, coupling, left, right, turned, lead, update_0, update_1, held, left_in, low_turned, sems):
    copies = [
        pltpu.make_async_copy(coupling.at[pl.ds(0, SUMMED)], held, sems.at[0]),
        pltpu.make_async_copy(left.at[pl.ds(0, SUMMED)], left_in, sems.at[1]),
    ]
    for copy in copies:
        copy.start()
    for level in range(1, SUMMED + 1):
        low_turned[(level - 1) * LANE : level * LANE, :] = right[level].T
    for copy in copies:
        copy.wait()
    block = masked_rows(pair_of(left_in, 0), live)
    gram = jnp.concatenate([dot(low_turned[...], block), dot(turned[...], block)], axis=0)
    for level, out in ((0, update_0), (1, update_1)):
        out[...] = updates_of_level(gram, 0, level, canonical(held, index, level))


def coefficient_kernel(live, order, fields, right, first_out, solve_out, tree):
    nvec = first_out.shape[0]
    points = order.shape[1]
    chunk = 256
    for low in range(0, points, chunk):
        moved = dot(fields[...], one_hot(order[...], low, chunk))
        slot = lax.broadcasted_iota(jnp.int32, moved.shape, 1) + low
        tree[:, low : low + chunk] = jnp.where(slot < live[0], moved, 0.0).astype(BF)
    for level in range(0, LEVELS, 2):
        pair = dot(tree[...], pair_of(right, level))
        for now in (level, level + 1):
            part = pair[:, (now - level) * LANE : (now - level + 1) * LANE] * scale(now)
            first_out[:, (now + 1) * LANE : (now + 2) * LANE] = part[:nvec].astype(BF)
            if now == 0:
                first_out[:, :LANE] = part[nvec:].astype(BF)
            else:
                solve_out[:, (now - 1) * LANE : now * LANE] = part[nvec:]


def canonical(coupling, index, level):
    held = coupling[level]
    swapped = jnp.concatenate([held[LANE:], held[:LANE]], axis=0)
    second = (lax.shift_right_logical(index[0], level) & 1) == 1
    return jnp.where(second, swapped, held)


def direct_kernel(order, tree, block, lead, prod_out, hot_out):
    points = order.shape[1]
    nvec = prod_out.shape[0]
    chunk = 256
    for low in range(0, points, chunk):
        hot_out[:, low : low + chunk] = one_hot(order[...], low, chunk)
    prod_out[...] = dot_t(tree[:nvec, :], block[...])


def masked_rows(block, live):
    rows = lax.broadcasted_iota(jnp.int32, block.shape, 0)
    return jnp.where(rows < live[0], block.astype(F32), 0.0).astype(BF)


def moved_kernel(live, hot, left, moved_out, left_cat, sems):
    copies = [
        pltpu.make_async_copy(left.at[level], columns(left_cat, level - BEFORE), sems.at[level - BEFORE])
        for level in range(BEFORE, LEVELS)
    ]
    for copy in copies:
        copy.start()
    for copy in copies:
        copy.wait()
    moved_out[...] = dot(hot[...], masked_rows(left_cat[...], live)).astype(BF)


def partial_kernel(live, index, coupling, left, tree, direct, hot, *rest):
    siblings, joined = rest[:BEFORE], rest[BEFORE : 2 * BEFORE]
    prod_out, sol_out, coupling_out, left_cat, sems = rest[2 * BEFORE :]
    copies = [
        pltpu.make_async_copy(left.at[level], columns(left_cat, level), sems.at[level])
        for level in range(BEFORE)
    ]
    for copy in copies:
        copy.start()
    for level in range(BEFORE, LEVELS):
        at = (level - BEFORE) * 2 * LANE
        coupling_out[at : at + 2 * LANE, :] = canonical(coupling, index, level)
    coupled = [dot(joined[level][...], canonical(coupling, index, level)).astype(BF) for level in range(BEFORE)]
    siblings = [block[...] for block in siblings]
    terms = jnp.concatenate([jnp.concatenate(siblings, axis=1), jnp.concatenate(coupled, axis=1)], axis=0)
    for copy in copies:
        copy.wait()
    terms = dot_t(terms, left_cat[...])
    nvec = direct.shape[0]
    total = jnp.concatenate([direct[...] + terms[:nvec], tree[nvec:, :].astype(F32) - terms[nvec:]], axis=0)
    slot = lax.broadcasted_iota(jnp.int32, total.shape, 1)
    total = jnp.where(slot < live[0], total, 0.0)
    high = total.astype(BF)
    low = (total - high.astype(F32)).astype(BF)
    both = dot_t(jnp.concatenate([high, low], axis=0), hot[...])
    prod_out[...] = both[:nvec] + both[2 * nvec : 3 * nvec]
    sol_out[...] = both[nvec : 2 * nvec] + both[3 * nvec :]


def last_kernel(coupling, moved, prod, sol, *rest):
    count = LEVELS - BEFORE
    siblings, joined, (prod_out, sol_out) = rest[:count], rest[count : 2 * count], rest[2 * count :]
    coupled = [
        dot(joined[at][...], coupling[2 * at * LANE : 2 * (at + 1) * LANE, :]).astype(BF) for at in range(count)
    ]
    siblings = [block[...] for block in siblings]
    terms = jnp.concatenate([jnp.concatenate(siblings, axis=1), jnp.concatenate(coupled, axis=1)], axis=0)
    terms = dot_t(terms, moved[...])
    nvec = prod.shape[0]
    prod_out[...] = prod[...] + terms[:nvec]
    sol_out[...] = sol[...] - terms[nvec:]


def params(mib):
    return pltpu.CompilerParams(vmem_limit_bytes=mib << 20)


def shape(rows, lanes, dtype=BF):
    return jax.ShapeDtypeStruct((rows, lanes), dtype)


def swap(block, mask):
    count = lax.axis_size("leaf") * lax.axis_size("sub")
    return lax.ppermute(block, ("leaf", "sub"), [(i, i ^ mask) for i in range(count)])


def cols(block, low, high=None):
    return block[:, low * LANE : None if high is None else high * LANE]


def cat(*blocks):
    return jnp.concatenate([block.astype(BF) for block in blocks], axis=1)


def in_hbm(block):
    return pltpu.with_memory_space_constraint(block, pltpu.HBM)


def behind(lead, *blocks):
    def kernel(lead_in, *refs):
        refs[-1][...] = sum(ref[...].astype(F32) for ref in refs[:-1]).astype(BF)

    return pl.pallas_call(
        kernel,
        out_shape=pltpu.VMEM(blocks[0].shape, BF),
        in_specs=[pl.BlockSpec(memory_space=pl.ANY)] + [VMEM] * len(blocks),
        out_specs=VMEM,
        compiler_params=params(4),
        cost_estimate=pl.CostEstimate(flops=1_000_000, bytes_accessed=200_000, transcendentals=0),
        name="behind",
    )(lead, *blocks)


def per_device(vectors, right_side, tree_order, live_counts, leaf_block, left_basis, right_bases, coupling):
    nvec, points = vectors.shape
    index = lax.axis_index("leaf") * lax.axis_size("sub") + lax.axis_index("sub")
    index_1 = index.astype(jnp.int32).reshape(1)
    coupling = coupling[0]

    def pick(level, if_set, if_clear):
        side = jnp.broadcast_to(bits[level : level + 1, : if_set.shape[1]], if_set.shape)
        return jnp.where(side > 0, if_set, if_clear)

    def join(mine, other, level):
        return cat(pick(level, other, mine), pick(level, mine, other))

    def whole_of(mine, theirs, cost=1):
        width = mine.shape[1] // 4

        def kernel(index_in, mine_in, theirs_in, out):
            second = (lax.shift_right_logical(index_in[0], 2) & 1) == 1
            for at in range(4):
                side = slice(at * width, (at + 1) * width)
                own, other = mine_in[:, side], theirs_in[:, side]
                out[at * nvec : (at + 1) * nvec, :] = jnp.where(second, other, own)
                out[(at + 4) * nvec : (at + 5) * nvec, :] = jnp.where(second, own, other)

        return pl.pallas_call(
            kernel,
            out_shape=pltpu.VMEM((8 * nvec, width), BF),
            in_specs=[SMEM, VMEM, VMEM],
            out_specs=VMEM,
            compiler_params=params(4),
            cost_estimate=pl.CostEstimate(flops=cost * 1_000_000_000, bytes_accessed=1_000_000, transcendentals=0),
            name="whole",
        )(index_1, mine, theirs)

    def by_sub(blocks):
        even = [pick(0, blocks[i ^ 1], blocks[i]) for i in range(4)]
        return [pick(1, even[i ^ 2], even[i]) for i in range(4)]

    summed = sum(LEVELS - 1 - level for level in range(SUMMED, LEVELS - 1))
    home, away, bits, order_in, fields, right_in, turned = pl.pallas_call(
        summed_kernel,
        out_shape=(pltpu.VMEM((LANE, summed * LANE), BF),) * 2
        + (pltpu.VMEM((LEVELS, 2 * points), F32), pltpu.VMEM((1, points), jnp.int32), pltpu.VMEM((2 * nvec, points), BF))
        + (pltpu.VMEM(right_bases.shape, BF), pltpu.VMEM(((LEVELS - 1 - SUMMED) * LANE, points), BF)),
        in_specs=[SMEM, SMEM] + [HBM] * 6,
        out_specs=(VMEM,) * 7,
        scratch_shapes=[
            pltpu.VMEM(coupling.shape, BF),
            pltpu.VMEM((LEVELS - 1 - SUMMED, points, LANE), BF),
            pltpu.SemaphoreType.DMA((2, LEVELS + 3)),
        ],
        compiler_params=params(20),
        cost_estimate=pl.CostEstimate(flops=1_500_000_000, bytes_accessed=5_000_000, transcendentals=0),
        name="summed",
    )(
        live_counts,
        index_1,
        *map(in_hbm, (tree_order, vectors, right_side, coupling, left_basis, right_bases)),
    )
    got = swap(away, 4)
    first, coef, tree = pl.pallas_call(
        coefficient_kernel,
        out_shape=(
            pltpu.VMEM((nvec, 9 * LANE), BF),
            pltpu.VMEM((nvec, 7 * LANE), F32),
            pltpu.VMEM((2 * nvec, points), BF),
        ),
        in_specs=[SMEM, VMEM, VMEM, VMEM],
        out_specs=(VMEM,) * 3,
        compiler_params=params(12),
        cost_estimate=pl.CostEstimate(flops=300_000_000, bytes_accessed=2_500_000, transcendentals=0),
        name="coefficients",
    )(live_counts, order_in, fields, right_in)
    halves = (home.astype(F32) + got.astype(F32)).astype(BF)
    piece = halves.shape[0] // 4
    rows_of = by_sub([halves[i * piece : (i + 1) * piece] for i in range(4)])

    siblings, joined = [], []

    sent = {1: cat(first, rows_of[1]), 2: rows_of[2], 3: rows_of[3]}
    update_0, update_1 = pl.pallas_call(
        own_kernel,
        out_shape=(pltpu.VMEM((2 * LANE, 7 * LANE), BF), pltpu.VMEM((2 * LANE, 6 * LANE), BF)),
        in_specs=[SMEM, SMEM, HBM, HBM, VMEM, VMEM, pl.BlockSpec(memory_space=pl.ANY)],
        out_specs=(VMEM, VMEM),
        scratch_shapes=[
            pltpu.VMEM((SUMMED, 2 * LANE, LANE), BF),
            pltpu.VMEM((SUMMED, points, LANE), BF),
            pltpu.VMEM((SUMMED * LANE, points), BF),
            pltpu.SemaphoreType.DMA((2,)),
        ],
        compiler_params=params(16),
        cost_estimate=pl.CostEstimate(flops=1_500_000_000, bytes_accessed=1_000_000, transcendentals=0),
        name="own",
    )(live_counts, index_1, in_hbm(coupling), in_hbm(left_basis), right_in, turned, sent[1])
    got = {mask: swap(sent[mask], mask) for mask in (1, 2, 3)}
    pieces = sum(
        block.astype(F32) for block in (rows_of[0], cols(got[1], 1 + LEVELS), got[2], got[3])
    ).astype(BF)
    joined.append(join(cols(first, 0, 1), cols(got[1], 0, 1), 0))
    siblings.append(cols(got[1], 1, 2))
    prod = cols(first, 2).astype(F32) + cols(got[1], 2, 1 + LEVELS).astype(F32)
    coef = coef - dot(joined[0], update_0)

    mine = cols(coef, 0, 1).astype(BF)
    got = {1: swap(mine, 1), 2: swap(mine, 2), 3: swap(cat(mine, prod), 3)}
    at = [sum(LEVELS - 1 - below for below in range(SUMMED, level)) for level in range(LEVELS)]
    upper = cols(pieces, at[3])
    near = swap(upper, 8)
    far = behind(upper, cols(pieces, at[4]))
    far = swap(far, 16).astype(F32) + swap(far, 24).astype(F32)
    upper = upper.astype(F32) + near.astype(F32)
    pieces = cat(cols(pieces, 0, at[3]), cols(upper, 0, at[4] - at[3]), cols(upper, at[4] - at[3]) + far)
    parts = {mask: cols(block, 0, 1).astype(F32) for mask, block in got.items()}
    joined.append(join((mine.astype(F32) + parts[1]).astype(BF), (parts[2] + parts[3]).astype(BF), 1))
    got_prod = cols(got[3], 1)
    siblings.append(cols(got_prod, 0, 1))
    prod = cols(prod, 1) + cols(got_prod, 1).astype(F32)
    coef = cols(coef, 1) - dot(joined[1], update_1)

    sent = cat(coef, pieces)
    direct, hot = pl.pallas_call(
        direct_kernel,
        out_shape=(pltpu.VMEM((nvec, points), F32), pltpu.VMEM((points, points), BF)),
        in_specs=[VMEM, VMEM, VMEM, pl.BlockSpec(memory_space=pl.ANY)],
        out_specs=(VMEM, VMEM),
        compiler_params=params(12),
        cost_estimate=pl.CostEstimate(flops=2_000_000_000, bytes_accessed=2_000_000, transcendentals=0),
        name="direct",
    )(tree_order, tree, leaf_block, sent)
    moved = pl.pallas_call(
        moved_kernel,
        out_shape=pltpu.VMEM((points, (LEVELS - BEFORE) * LANE), BF),
        in_specs=[SMEM, VMEM, HBM],
        out_specs=VMEM,
        scratch_shapes=[
            pltpu.VMEM((points, (LEVELS - BEFORE) * LANE), BF),
            pltpu.SemaphoreType.DMA((LEVELS - BEFORE,)),
        ],
        compiler_params=params(12),
        cost_estimate=pl.CostEstimate(flops=1_500_000_000, bytes_accessed=2_000_000, transcendentals=0),
        name="moved",
    )(live_counts, hot, left_basis)
    got = {mask: swap(sent, mask) for mask in (1, 3, 2)}
    got[0] = sent
    lead = LEVELS - SUMMED
    total = sum(cols(got[mask], 0, lead).astype(F32) for mask in (0, 1, 3, 2))
    quarters = by_sub([cols(got[mask], lead) for mask in range(4)])
    total, moved, direct = lax.optimization_barrier((total, moved, direct))

    early = [cols(quarter, 0, at[5]) for quarter in quarters]
    sent = cat(total, prod, *early)
    late = cat(*(cols(quarter, at[5]) for quarter in quarters))

    def from_four(block, low, high):
        width = block.shape[1] // (4 * LANE)
        return cat(*(cols(block, i * width + low, i * width + high) for i in range(4)))

    def exchange(level, mask, sent, total, prod):
        left_over = LEVELS - level
        got = swap(sent, mask)
        got_total, got_prod = cols(got, 0, left_over), cols(got, left_over, 2 * left_over)
        joined.append(join(cols(sent, 0, 1), cols(got_total, 0, 1), level))
        siblings.append(cols(got_prod, 0, 1))
        prod = cols(prod, 1) + cols(got_prod, 1).astype(F32)
        return cols(total, 1) + cols(got_total, 1).astype(F32), prod, cols(got, 2 * left_over)

    def apply(level, total):
        return total - dot(joined[level], updates_of[level])

    total, prod, theirs = exchange(2, 4, sent, total, prod)
    whole = whole_of(cat(*early), theirs)
    updates_of = {level: cols(whole, at[level], at[level + 1]) for level in (2, 3, 4)}
    total = apply(2, total)

    sent = cat(total, prod)
    late = behind(sent, late)
    got_late = swap(late, 32)
    total, prod, _ = exchange(3, 8, sent, total, prod)
    total = apply(3, total)

    sent = cat(total, prod)
    late = behind(sent, late, got_late)
    own = from_four(late, 0, 2)
    updates_of[5] = whole_of(own, swap(own, 4))
    got_late = swap(late, 64)
    total, prod, _ = exchange(4, 24, sent, total, prod)
    total = apply(4, total)

    sent = cat(total, prod)
    far = behind(sent, got_late)
    last = from_four(late, 2, 3).astype(F32) + from_four(far, 2, 3).astype(F32)
    own = cat(from_four(far, 0, 2), last)
    theirs = swap(own, 4)
    far_update, updates_of[6] = whole_of(cols(own, 0, 8), cols(theirs, 0, 8)), whole_of(cols(own, 8), cols(theirs, 8))
    part_prod, part_sol, last_coupling = pl.pallas_call(
        partial_kernel,
        out_shape=(pltpu.VMEM((nvec, points), F32),) * 2
        + (pltpu.VMEM(((LEVELS - BEFORE) * 2 * LANE, LANE), BF),),
        in_specs=[SMEM, SMEM, VMEM, HBM] + [VMEM] * (3 + 2 * BEFORE),
        out_specs=(VMEM,) * 3,
        scratch_shapes=[
            pltpu.VMEM((points, BEFORE * LANE), BF),
            pltpu.SemaphoreType.DMA((BEFORE,)),
        ],
        compiler_params=params(12),
        cost_estimate=pl.CostEstimate(flops=2_000_000_000, bytes_accessed=3_000_000, transcendentals=0),
        name="partial",
    )(live_counts, index_1, coupling, left_basis, tree, direct, hot, *siblings, *joined)
    got = [sent] + [swap(sent, mask) for mask in (32, 64, 96)]
    sums = []
    for low, update in ((0, updates_of[5]), (2, far_update)):
        pair = join(cols(got[low], 0, 1), cols(got[low + 1], 0, 1), 5)
        if low == 0:
            joined.append(pair)
        both = [cols(block, 1, 3).astype(F32) for block in got[low : low + 2]]
        sums.append(both[0] + both[1] - dot(pair, update))
    joined.append(join(cols(sums[0], 0, 1).astype(BF), cols(sums[1], 0, 1).astype(BF), 6))
    total = cols(sums[0], 1) + cols(sums[1], 1) - dot(joined[6], updates_of[6])
    siblings.append(cols(got[1], 3, 4))
    siblings.append((cols(got[2], 4, 5).astype(F32) + cols(got[3], 4, 5).astype(F32)).astype(BF))
    prod = sum(cols(block, 5).astype(F32) for block in got)
    total, part_prod, part_sol = lax.optimization_barrier((total, part_prod, part_sol))

    exchange(7, 192, cat(total, prod), total, prod)
    return pl.pallas_call(
        last_kernel,
        out_shape=(shape(nvec, points, F32),) * 2,
        in_specs=[VMEM] * (4 + 2 * (LEVELS - BEFORE)),
        out_specs=(VMEM, VMEM),
        compiler_params=params(8),
        cost_estimate=pl.CostEstimate(flops=30_000_000, bytes_accessed=1_000_000, transcendentals=0),
        name="last",
    )(last_coupling, moved, part_prod, part_sol, *siblings[BEFORE:], *joined[BEFORE:])


def solution(mesh):
    placed = (
        P(None, ("leaf", "sub")),
        P(None, ("leaf", "sub")),
        P(("leaf", "sub"), None),
        P(("leaf", "sub")),
        P(("leaf", "sub"), None),
        P(None, ("leaf", "sub"), None),
        P(None, ("leaf", "sub"), None),
        P(("leaf", "sub"), None, None, None),
    )
    return jax.shard_map(
        per_device,
        mesh=mesh,
        in_specs=placed,
        out_specs=(P(None, ("leaf", "sub")), P(None, ("leaf", "sub"))),
        check_vma=False,
    )
```
